256 devices in a mesh: adapter: 32 (over x, z), seq: 8 (over y, core).
Axes of the slice: x: 4, y: 4, z: 8, core: 2. Of those that a mesh axis runs over, the one named last changes fastest.
Arguments:
- tokens: bfloat16 [32768, 8192], P('adapter', 'seq'), may hold values from -6 to 6
- frozen_weight: bfloat16 [8192, 1024], P('seq'), may hold values from -0.0625 to 0.0625
- saved_mid: bfloat16 [32768, 128], P(('adapter', 'seq')), may hold values from -6 to 6
- cotangent: bfloat16 [32768, 1024], P('adapter', 'seq'), may hold values from -0.059814453 to 0.059814453
- up_stack: bfloat16 [32, 128, 1024], P(None, None, 'seq'), may hold values from -0.5 to 0.5
- block_job: int32 [256, 1], P('adapter'), may hold values from 0 to 31; in each aligned block of 8 rows (0 to 7, 8 to 15, ...) no two rows name the same one
- block_fill: int32 [256], P('adapter'), may hold values from 1 to 128
- slot_of: int32 [32], replicated, may hold values from 0 to 31, each once
Outputs:
- keys: bfloat16 [32768, 1024], P(('adapter', 'seq'))
- grad_down: float32 [32, 8192, 128], P('adapter', 'seq')
- grad_up: float32 [32, 128, 1024], P('adapter', None, 'seq')
The draws below stay inside these ranges and needn't reach their ends.
Inputs may be any that keep to these rules, and one draw needn't show every extreme that they name: `block_job`: within each aligned run of 8 blocks no adapter id appears twice. `slot_of`: each slot holds exactly one adapter.
All inputs are finite; a program needn't handle non-finite values.
Results may differ from the reference program's by a relative error of at most 0.0029.
Values may be sent and summed in bfloat16 or wider, within the bound.
No kernel may reach another device: no remote copies, remote signals or barrier semaphores. Data moves between devices by JAX's collectives and lax.ppermute only.
A program may use at most 128 MiB of HBM per device.

```python
import math
import jax
import jax.numpy as jnp
import numpy as np
from jax import lax

D = 8192
KEY_FEATURE_WIDTH = 1024
R = 128
BLK = 128
ADAPTERS = 32
TOKENS = 32768
BLOCKS = 256
GROUP_BLOCKS = 8


def draw_block_fill(key, part):
    key = jax.random.fold_in(key, 7)
    first_key, second_key = jax.random.split(key)
    fills = jax.random.randint(first_key, (BLOCKS,), 1, BLK + 1)
    where_full = jax.random.randint(second_key, (), 0, BLOCKS)
    return fills.at[where_full].set(BLK).astype(jnp.int32)


def block_levels(key, dims, shards, low, high):
    def one(axis_at, blocks):
        heights = jax.random.uniform(jax.random.fold_in(jax.random.fold_in(key, 6), axis_at), (blocks,), jnp.float32, low / len(shards), high / len(shards))
        return jnp.repeat(jnp.exp(heights), dims[axis_at] // blocks).reshape((-1,) + (1,) * (len(dims) - axis_at - 1))

    loudness = one(*shards[0])
    for cut in shards[1:]:
        loudness = loudness * one(*cut)
    return loudness


def assign_block(stream_key, own, number, rows, number_of, top, most, slope):
    ranking = jax.random.permutation(stream_key, number_of)
    crowded, ordinary = portions_of(number_of, rows * top, most, slope, True), portions_of(number_of, rows * top, most, slope, False)
    places = jnp.arange(number_of)

    def named(lengths, rotation):
        used = int((lengths > 0).sum())
        fixed = max(1, used // 4)
        passed = fixed + (places - fixed + rotation * (used - fixed)) % max(1, number_of - fixed)
        return jnp.zeros((number_of,), jnp.int32).at[ranking[jnp.where(places < fixed, places, passed)]].set(jnp.asarray(lengths, jnp.int32))

    lengths = jnp.where(number % 4 == 0, named(crowded, number // 4), named(ordinary, number - number // 4 - 1))
    mixed = jax.random.permutation(jax.random.fold_in(own, 3), number_of)
    giver, receiver = mixed[0:number_of // 2 * 2:2], mixed[1:number_of // 2 * 2:2]
    margin = jnp.minimum(lengths[giver] - 1, most - lengths[receiver]) // 2
    margin = jnp.where((giver == ranking[0]) | (receiver == ranking[0]) | (lengths[receiver] == 0), 0, jnp.maximum(margin, 0))
    passed = jax.random.randint(jax.random.fold_in(own, 4), (number_of // 2,), 0, 1 << 20) % (margin + 1)
    lengths = lengths.at[giver].add(-passed).at[receiver].add(passed)
    labels = jnp.searchsorted(jnp.cumsum(lengths), jnp.arange(rows * top), side="right").astype(jnp.int32)
    grid = labels.reshape(top, rows).T
    grid = grid[jax.random.permutation(jax.random.fold_in(own, 1), rows)]
    rotation = jax.random.randint(jax.random.fold_in(own, 2), (rows, 1), 0, top)
    return jnp.take_along_axis(grid, (jnp.arange(top)[None, :] + rotation) % top, axis=1)


def portions_of(number_of, total, reach, lean, full):
    loads = [(1 << 20) // math.isqrt(standing ** lean) + 1 for standing in range(1, number_of + 1)]
    largest = reach if full else min(reach, max(-(-total // number_of), total * loads[0] // sum(loads)))
    least = 1 if total - largest >= number_of - 1 else 0
    counts, spare = [largest] + [least] * (number_of - 1), total - largest - least * (number_of - 1)
    while spare > 0:
        movable = [i for i in range(1, number_of) if counts[i] < largest] or [i for i in range(1, number_of) if counts[i] < reach]
        whole, budget = sum([loads[i] for i in movable]), spare
        for i in movable:
            addition = min(reach - counts[i], max(1, budget * loads[i] // whole), spare)
            counts[i] = counts[i] + addition
            spare = spare - addition
    return np.array(counts)


def bell_draw(stream_key, extent, width, most, cuts=(), dtype=jnp.bfloat16):
    result = width * jax.random.normal(stream_key, extent, jnp.float32)
    if cuts:
        result = result * block_levels(stream_key, extent, cuts, -0.22, 0.18)
    return jnp.clip(result, -most, most).astype(dtype)


def setup_inputs(seed: int = 0) -> dict:
    splits = jax.random.split(jax.random.key(seed), 9)
    tokens = bell_draw(splits[0], (TOKENS, D), 1.0, 6.0, ((0, 32), (1, 8)))
    frozen_weight = bell_draw(splits[1], (D, KEY_FEATURE_WIDTH), D ** -0.5, 0.0625, ((0, 8),))
    saved_mid = bell_draw(splits[2], (TOKENS, R), 1.0, 6.0, ((0, 256),))
    cotangent = bell_draw(splits[3], (TOKENS, KEY_FEATURE_WIDTH), 0.01, 0.059814453, ((0, 32), (1, 8)))
    up_stack = bell_draw(splits[4], (ADAPTERS, R, KEY_FEATURE_WIDTH), R ** -0.5, 0.5, ((2, 8),))
    block_job_keys = jax.random.split(jax.random.fold_in(splits[5], 1), BLOCKS // GROUP_BLOCKS)
    block_job_turns = jax.random.permutation(jax.random.fold_in(splits[5], 3), BLOCKS // GROUP_BLOCKS)
    block_job = jax.vmap(lambda own, number: assign_block(jax.random.fold_in(splits[5], 2), own, number, GROUP_BLOCKS, ADAPTERS, 1, 1, 2))(block_job_keys, block_job_turns).reshape((BLOCKS, 1))
    block_fill = draw_block_fill(jax.random.fold_in(splits[8], 71), 0)
    slot_of = jax.random.permutation(splits[7], ADAPTERS).astype(jnp.int32)
    return dict(tokens=tokens, frozen_weight=frozen_weight, saved_mid=saved_mid, cotangent=cotangent, up_stack=up_stack, block_job=block_job, block_fill=block_fill, slot_of=slot_of)


ADAPTER_SCALE = 2.0


def reference(tokens, frozen_weight, saved_mid, cotangent, up_stack, block_job, block_fill, slot_of):
    blocks = tokens.shape[0] // BLK
    jobs = block_job[:, 0]
    picked_adapter = jnp.take(up_stack, jobs, axis=0).astype(jnp.float32)
    middle_blocks = saved_mid.reshape(blocks, BLK, R)
    adapter_output = ADAPTER_SCALE * jnp.einsum('axk,aky->axy', middle_blocks.astype(jnp.float32), picked_adapter)
    frozen_output = jnp.dot(tokens, frozen_weight, preferred_element_type=jnp.float32)
    keys = (frozen_output + adapter_output.reshape(-1, KEY_FEATURE_WIDTH)).astype(jnp.bfloat16)
    position = lax.broadcasted_iota(jnp.int32, (blocks, BLK), 1)
    validity = (position < block_fill[:, None]).astype(jnp.bfloat16)
    grad_blocks = cotangent.reshape(blocks, BLK, KEY_FEATURE_WIDTH) * validity[:, :, None]
    mid_grad = jnp.einsum('nbc,nrc->nbr', grad_blocks.astype(jnp.float32), picked_adapter).astype(jnp.bfloat16)
    slots = jnp.take(slot_of, jobs).astype(jnp.int32)
    token_blocks = tokens.reshape(blocks, BLK, D)

    def add_block(index, carry):
        down_sum, up_sum = carry
        slot_index = slots[index].astype(jnp.int32)
        down_term = ADAPTER_SCALE * jnp.dot(token_blocks[index].T, mid_grad[index], preferred_element_type=jnp.float32)
        up_term = ADAPTER_SCALE * jnp.dot(middle_blocks[index].T, grad_blocks[index], preferred_element_type=jnp.float32)
        down_old = lax.dynamic_index_in_dim(down_sum, slot_index, 0, True)
        up_old = lax.dynamic_index_in_dim(up_sum, slot_index, 0, True)
        down_sum = lax.dynamic_update_slice_in_dim(down_sum, down_old + down_term[None], slot_index, 0)
        up_sum = lax.dynamic_update_slice_in_dim(up_sum, up_old + up_term[None], slot_index, 0)
        return down_sum, up_sum

    down_start = jnp.zeros((ADAPTERS, D, R), jnp.float32)
    up_start = jnp.zeros((ADAPTERS, R, KEY_FEATURE_WIDTH), jnp.float32)
    grad_down, grad_up = lax.fori_loop(0, blocks, add_block, (down_start, up_start))
    return keys, grad_down, grad_up
```

```python
import jax
import jax.numpy as jnp
from jax import lax
from jax.experimental import pallas as pl
from jax.experimental.pallas import tpu as pltpu
from jax.sharding import Mesh, PartitionSpec as P

BLK = 128
ADAPTER_SCALE = 2.0
SEQ = ("y", "core")


def slot_sums(slots, token_parts, mids, up_parts, slot_count):
    groups, blocks, rows, width = token_parts.shape
    rank = mids.shape[-1]
    up_rows = up_parts.shape[2]

    def kernel(slots_ref, tokens_ref, mids_ref, up_ref, out_ref, acc):
        acc[...] = jnp.zeros_like(acc)
        for g in range(groups):
            for b in range(blocks):
                slot = slots_ref[g, b]
                acc[slot, :width] += lax.dot_general(
                    tokens_ref[g, b],
                    mids_ref[b, g],
                    (((0,), (0,)), ((), ())),
                    preferred_element_type=jnp.float32,
                )
                acc[slot, width:] += up_ref[g, b].astype(jnp.float32)
        out_ref[...] = acc[...].astype(out_ref.dtype)

    vmem = pl.BlockSpec(memory_space=pltpu.VMEM)
    return pl.pallas_call(
        kernel,
        out_shape=jax.ShapeDtypeStruct((slot_count, width + up_rows, rank), jnp.bfloat16),
        in_specs=[pl.BlockSpec(memory_space=pltpu.SMEM), vmem, vmem, vmem],
        out_specs=vmem,
        scratch_shapes=[pltpu.VMEM((slot_count, width + up_rows, rank), jnp.float32)],
        compiler_params=pltpu.CompilerParams(vmem_limit_bytes=32 * 1024 * 1024),
    )(slots, token_parts, mids, up_parts)


def per_device(
    tokens, frozen_weight, saved_mid, cotangent, up_stack, block_job, block_fill, slot_of
):
    rows, width = tokens.shape
    features = cotangent.shape[1]
    rank = saved_mid.shape[1]
    nblocks = block_job.shape[0]
    slot_count = slot_of.shape[0]
    nx, nz = lax.axis_size("x"), lax.axis_size("z")
    bf16, f32 = jnp.bfloat16, jnp.float32
    jobs = block_job[:, 0]

    with jax.named_scope("tokens_over_z"):
        token_parts = lax.all_to_all(tokens, "z", split_axis=1, concat_axis=0, tiled=True)
        token_parts = token_parts.reshape(nz, nblocks, BLK, width // nz)

    with jax.named_scope("mid_sums"):
        picked = jnp.take(up_stack, jobs, axis=0)
        position = lax.broadcasted_iota(jnp.int32, (nblocks, BLK), 1)
        validity = (position < block_fill[:, None]).astype(bf16)
        grad_blocks = cotangent.reshape(nblocks, BLK, features) * validity[:, :, None]
        mid_partial = jnp.einsum("nbc,nrc->nbr", grad_blocks, picked, preferred_element_type=f32)
        high = lax.reduce_precision(mid_partial, exponent_bits=8, mantissa_bits=7)
        low = (mid_partial - high).astype(bf16)
        own_saved = jnp.broadcast_to(saved_mid[None], (nblocks, BLK, rank))
        sent = jnp.concatenate([high.astype(bf16), low, own_saved], axis=1)
        got = lax.all_to_all(sent, SEQ, split_axis=0, concat_axis=0, tiled=True)
        mid_grad = jnp.sum(got[:, : 2 * BLK].astype(f32).reshape(-1, BLK, rank), axis=0).astype(bf16)
        saved_blocks = got[:, 2 * BLK :]

    with jax.named_scope("mid_gather"):
        slots = jnp.take(slot_of, jobs)
        slot_rows = jnp.broadcast_to(
            jnp.pad(slots.astype(bf16), (0, rank - nblocks))[None], (16, rank)
        )
        column = lax.all_gather(jnp.concatenate([mid_grad, slot_rows], axis=0), "z", axis=0)
        column_slots = column[:, BLK, :nblocks].astype(jnp.int32)
        mids = lax.all_gather(column[:, :BLK], SEQ, axis=0)

    with jax.named_scope("up_over_z"):
        up_terms = jnp.einsum("nbr,nbc->nrc", saved_blocks, grad_blocks, preferred_element_type=f32)
        up_parts = lax.all_to_all(up_terms.astype(bf16), "z", split_axis=1, concat_axis=0, tiled=True)
        up_parts = up_parts.reshape(nz, nblocks, rank // nz, features)

    with jax.named_scope("keys"):
        adapter_output = ADAPTER_SCALE * jnp.einsum(
            "axk,aky->axy", saved_blocks, picked, preferred_element_type=f32
        ).reshape(rows, features)
        column_offset = lax.axis_index(SEQ) * features
        frozen_output = jnp.dot(tokens, frozen_weight, preferred_element_type=f32)
        middle = lax.dynamic_slice_in_dim(frozen_output, column_offset, features, 1) + adapter_output
        keys = lax.psum_scatter(
            lax.dynamic_update_slice_in_dim(frozen_output, middle, column_offset, 1),
            SEQ,
            scatter_dimension=0,
            tiled=True,
        ).astype(bf16)

    with jax.named_scope("slot_sums"):
        sums = slot_sums(column_slots, token_parts, mids, up_parts, slot_count)

    with jax.named_scope("sums_over_x"):
        over_x = lax.all_to_all(sums, "x", split_axis=0, concat_axis=0, tiled=True)
        over_x = over_x.reshape(nx, nz, -1, rank)
        totals = ADAPTER_SCALE * jnp.sum(over_x.astype(f32), axis=0)
    with jax.named_scope("totals_over_z"):
        owned = lax.all_to_all(totals, "z", split_axis=0, concat_axis=0, tiled=True)
        split = width // nz
        grad_down = owned[:, :split].reshape(1, width, rank)
        grad_up = owned[:, split:].reshape(1, rank, features)
    return (keys, grad_down, grad_up)


def solution(mesh):
    chips = Mesh(mesh.devices.reshape(4, 8, 4, 2), ("x", "z", "y", "core"))
    adapter = ("x", "z")
    return jax.shard_map(
        per_device,
        mesh=chips,
        in_specs=(
            P(adapter, SEQ),
            P(SEQ, None),
            P(adapter + SEQ, None),
            P(adapter, SEQ),
            P(None, None, SEQ),
            P(adapter, None),
            P(adapter),
            P(),
        ),
        out_specs=(
            P(adapter + SEQ, None),
            P(adapter, SEQ, None),
            P(adapter, None, SEQ),
        ),
        check_vma=False,
    )
```

```python
import jax
import jax.numpy as jnp
from jax import lax
from jax.experimental import pallas as pl
from jax.experimental.pallas import tpu as pltpu
from jax.sharding import Mesh, PartitionSpec as P

BLK = 128
ADAPTER_SCALE = 2.0
SEQ = ("y", "core")
FIRST = ("x", "zp")
ADAPTER = ("x", "zq", "zp")
SLOT_ROWS = 16
LIMIT = pltpu.CompilerParams(vmem_limit_bytes=16 * 1024 * 1024)
WHOLE = pltpu.CompilerParams(vmem_limit_bytes=60 * 1024 * 1024)
VMEM = pl.BlockSpec(memory_space=pltpu.VMEM)
SMEM = pl.BlockSpec(memory_space=pltpu.SMEM)
HBM = pl.BlockSpec(memory_space=pltpu.HBM)
BF16 = jnp.bfloat16
F32 = jnp.float32


def shift(value, axis, distance):
    size = lax.axis_size(axis)
    return lax.ppermute(value, axis, [(i, (i + distance) % size) for i in range(size)])


def contract(left, right, left_dim, right_dim):
    return lax.dot_general(
        left, right, (((left_dim,), (right_dim,)), ((), ())), preferred_element_type=F32
    )


def masked(cot_ref, fill_ref, b):
    block = cot_ref[b * BLK : (b + 1) * BLK, :]
    position = lax.broadcasted_iota(jnp.int32, block.shape, 0)
    return jnp.where(position < fill_ref[b], block, jnp.zeros_like(block))


def mid_partials(place, jobs, fills, up_stack, cotangent):
    nblocks = jobs.shape[0]
    rank, features = up_stack.shape[1:]

    def kernel(place_ref, jobs_ref, fill_ref, up_ref, cot_ref, own_ref, other_ref, picked_ref, sems):
        copies = [
            pltpu.make_async_copy(up_ref.at[jobs_ref[b]], picked_ref.at[b], sems.at[b])
            for b in range(nblocks)
        ]
        for copy in copies:
            copy.start()
        core = place_ref[1]
        for pair in range(nblocks // 2):
            partials = []
            for b in (2 * pair, 2 * pair + 1):
                copies[b].wait()
                partials.append(contract(masked(cot_ref, fill_ref, b), picked_ref[b], 1, 1))
            own_ref[pair] = jnp.where(core == 0, partials[0], partials[1])
            other_ref[pair] = jnp.where(core == 0, partials[1], partials[0])

    half = jax.ShapeDtypeStruct((nblocks // 2, BLK, rank), F32)
    return pl.pallas_call(
        kernel,
        out_shape=[half, half, jax.ShapeDtypeStruct((nblocks, rank, features), BF16)],
        in_specs=[SMEM, SMEM, SMEM, HBM, VMEM],
        out_specs=[VMEM, VMEM, VMEM],
        scratch_shapes=[pltpu.SemaphoreType.DMA((nblocks,))],
        compiler_params=WHOLE,
        name="mid_partials",
    )(place, jobs, fills, up_stack, cotangent)


def y_payload(place, own, received, saved, saved_other):
    half, _, rank = own.shape

    def kernel(place_ref, own_ref, received_ref, saved_ref, saved_other_ref, keep_ref, out_ref):
        core = place_ref[1]
        first, second = saved_ref[...], saved_other_ref[...]
        out_ref[2 * half] = jnp.where(core == 0, first, second)
        out_ref[2 * half + 1] = jnp.where(core == 0, second, first)
        total = own_ref[...] + received_ref[...]
        keep_ref[...] = total
        high = total.astype(BF16)
        out_ref[:half] = high
        out_ref[half : 2 * half] = (total - high.astype(F32)).astype(BF16)

    return pl.pallas_call(
        kernel,
        out_shape=[
            jax.ShapeDtypeStruct((half, BLK, rank), F32),
            jax.ShapeDtypeStruct((2 * half + 2, BLK, rank), BF16),
        ],
        in_specs=[SMEM] + [VMEM] * 4,
        out_specs=[VMEM] * 2,
        compiler_params=LIMIT,
        name="y_payload",
    )(place, own, received, saved, saved_other)


def mid_grads(place, keep, sent, received):
    half, _, rank = keep.shape
    ny = len(received) + 1

    def kernel(place_ref, keep_ref, sent_ref, *refs):
        got = refs[: ny - 1]
        mids_ref, rows_ref = refs[ny - 1 :]
        y = place_ref[0]
        total = keep_ref[...]
        for ref in got:
            total += ref[:half].astype(F32) + ref[half : 2 * half].astype(F32)
        mids_ref[...] = total.astype(BF16)
        for d, ref in enumerate((sent_ref,) + got):
            source = lax.rem(y + ny - d, ny)
            rows_ref[2 * source] = ref[2 * half]
            rows_ref[2 * source + 1] = ref[2 * half + 1]

    return pl.pallas_call(
        kernel,
        out_shape=[
            jax.ShapeDtypeStruct((half, BLK, rank), BF16),
            jax.ShapeDtypeStruct((2 * half, BLK, rank), BF16),
        ],
        in_specs=[SMEM] + [VMEM] * (ny + 1),
        out_specs=[VMEM] * 2,
        compiler_params=LIMIT,
        name="mid_grads",
    )(place, keep, sent, *received)


def products(place, jobs, fills, slot_of, tokens, mids, mids_other, saved_rows, cotangent, parts):
    width = tokens.shape[1]
    nblocks, _, rank = saved_rows.shape
    part, split = width // parts, rank // parts
    height = part + split

    def kernel(
        place_ref, jobs_ref, fill_ref, slot_ref, tokens_ref, mids_ref, other_ref, saved_ref, cot_ref, out_ref
    ):
        core = place_ref[1]
        row = lax.broadcasted_iota(jnp.int32, (SLOT_ROWS, rank), 0)
        slots = jnp.zeros((SLOT_ROWS, rank), jnp.int32)
        for b in range(nblocks):
            slots = jnp.where(row == b, slot_ref[jobs_ref[b]], slots)
        slots = slots.astype(F32).astype(BF16)
        for i in range(parts):
            out_ref[i, nblocks * height :, :] = slots
        for b in range(nblocks):
            mine, other = mids_ref[b // 2], other_ref[b // 2]
            mid = jnp.where(core == b % 2, mine, other)
            up = contract(saved_ref[b], masked(cot_ref, fill_ref, b), 0, 0).astype(BF16)
            first = b * height
            for i in range(parts):
                block = tokens_ref[b * BLK : (b + 1) * BLK, i * part : (i + 1) * part]
                out_ref[i, first : first + part, :] = contract(block, mid, 0, 0).astype(BF16)
                out_ref[i, first + part : first + height, :] = up[i * split : (i + 1) * split]

    return pl.pallas_call(
        kernel,
        out_shape=jax.ShapeDtypeStruct((parts, nblocks * height + SLOT_ROWS, rank), BF16),
        in_specs=[SMEM] * 4 + [VMEM] * 5,
        out_specs=VMEM,
        compiler_params=LIMIT,
        name="products",
    )(place, jobs, fills, slot_of, tokens, mids, mids_other, saved_rows, cotangent)


def slot_sums(slots, terms, slot_count):
    groups, nblocks = slots.shape
    rank = terms.shape[2]
    height = (terms.shape[1] - SLOT_ROWS) // nblocks

    def kernel(slots_ref, terms_ref, out_ref, acc):
        acc[...] = jnp.zeros_like(acc)
        for g in range(groups):
            for b in range(nblocks):
                acc[slots_ref[g, b]] += terms_ref[g, b * height : (b + 1) * height, :].astype(F32)
        out_ref[...] = acc[...].astype(BF16)

    return pl.pallas_call(
        kernel,
        out_shape=jax.ShapeDtypeStruct((slot_count, height, rank), BF16),
        in_specs=[SMEM, VMEM],
        out_specs=VMEM,
        scratch_shapes=[pltpu.VMEM((slot_count, height, rank), F32)],
        compiler_params=LIMIT,
        name="slot_sums",
    )(slots, terms)


def finish(owned, part):
    nx, nq, npair, height, rank = owned.shape
    parts, split = nx * npair, height - part

    def kernel(owned_ref, down_ref, up_ref):
        for x in range(nx):
            for p in range(npair):
                total = owned_ref[x, 0, p].astype(F32)
                for q in range(1, nq):
                    total += owned_ref[x, q, p].astype(F32)
                total = ADAPTER_SCALE * total
                down_ref[x * npair + p] = total[:part]
                up_ref[x * npair + p] = total[part:]

    return pl.pallas_call(
        kernel,
        out_shape=[
            jax.ShapeDtypeStruct((parts, part, rank), F32),
            jax.ShapeDtypeStruct((parts, split, rank), F32),
        ],
        in_specs=[VMEM],
        out_specs=[VMEM, VMEM],
        compiler_params=LIMIT,
        name="finish",
    )(owned)


def keys_partials(place, tokens, frozen_weight, saved_rows, picked):
    rows, width = tokens.shape
    nblocks, rank, features = picked.shape
    half = nblocks // 2
    total = frozen_weight.shape[1]

    def block_of(i, j, place_ref):
        return 2 * j + lax.rem(place_ref[1] + i, 2)

    def kernel(place_ref, tokens_ref, weight_ref, saved_ref, picked_ref, own_ref, other_ref):
        columns = pl.ds(pl.multiple_of((2 * place_ref[0] + place_ref[1]) * features, features), features)
        for i, out_ref in enumerate((own_ref, other_ref)):

            @pl.when(pl.program_id(0) == i)
            def _():
                out_ref[0] = jnp.dot(tokens_ref[...], weight_ref[...], preferred_element_type=F32)
                out_ref[0, :, columns] += ADAPTER_SCALE * jnp.dot(
                    saved_ref[0], picked_ref[0], preferred_element_type=F32
                )

    shape = jax.ShapeDtypeStruct((half, BLK, total), F32)
    return pl.pallas_call(
        kernel,
        grid_spec=pltpu.PrefetchScalarGridSpec(
            num_scalar_prefetch=1,
            grid=(2, half),
            in_specs=[
                pl.BlockSpec((BLK, width), lambda i, j, place: (block_of(i, j, place), 0)),
                pl.BlockSpec((width, total), lambda i, j, place: (0, 0)),
                pl.BlockSpec((1, BLK, rank), lambda i, j, place: (block_of(i, j, place), 0, 0)),
                pl.BlockSpec((1, rank, features), lambda i, j, place: (block_of(i, j, place), 0, 0)),
            ],
            out_specs=[
                pl.BlockSpec((1, BLK, total), lambda i, j, place: (jnp.where(i == 0, j, half - 1), 0, 0)),
                pl.BlockSpec((1, BLK, total), lambda i, j, place: (jnp.where(i == 0, 0, j), 0, 0)),
            ],
        ),
        out_shape=[shape, shape],
        compiler_params=LIMIT,
        name="keys_partials",
    )(place, tokens, frozen_weight, saved_rows, picked)


def keys_chip_sums(place, own, received):
    ny, block, total = own.shape

    def kernel(place_ref, own_ref, received_ref, *outs):
        for d in range(ny):
            to = lax.rem(place_ref[0] + d, ny)
            outs[d][...] = own_ref[to] + received_ref[to]

    return pl.pallas_call(
        kernel,
        out_shape=[jax.ShapeDtypeStruct((block, total), F32)] * ny,
        in_specs=[SMEM, VMEM, VMEM],
        out_specs=[VMEM] * ny,
        compiler_params=LIMIT,
        name="keys_chip_sums",
    )(place, own, received)


def per_device(
    tokens, frozen_weight, saved_mid, cotangent, up_stack, block_job, block_fill, slot_of
):
    width = tokens.shape[1]
    features = cotangent.shape[1]
    rank = saved_mid.shape[1]
    nblocks = block_job.shape[0]
    slot_count = slot_of.shape[0]
    nx, nq, npair, ny = (lax.axis_size(name) for name in ADAPTER + ("y",))
    parts = nx * npair
    part, split = width // parts, rank // parts
    jobs = block_job.reshape(nblocks)
    place = jnp.stack([lax.axis_index(name) for name in SEQ]).astype(jnp.int32)

    with jax.named_scope("mid_sums"):
        saved_other = shift(saved_mid, "core", 1)
        own, other, picked = mid_partials(place, jobs, block_fill, up_stack, cotangent)
        keep, sent = y_payload(place, own, shift(other, "core", 1), saved_mid, saved_other)
        received = [shift(sent, "y", d) for d in range(1, ny)]
        mids, saved_rows = mid_grads(place, keep, sent, received)
        mids_other = shift(mids, "core", 1)
    with jax.named_scope("terms_over_first"):
        terms = products(
            place, jobs, block_fill, slot_of, tokens, mids, mids_other, saved_rows, cotangent, parts
        )
        terms = lax.all_to_all(terms, FIRST, split_axis=0, concat_axis=0, tiled=True)
        tail = nblocks * (part + split)
        slots = terms[:, tail : tail + nblocks, 0].astype(jnp.int32)
    with jax.named_scope("keys_core"):
        keys_own, keys_other = keys_partials(place, tokens, frozen_weight, saved_rows, picked)
        keys_parts = keys_chip_sums(place, keys_own, shift(keys_other, "core", 1))
    with jax.named_scope("keys_y"):
        keys = keys_parts[0]
        for d in range(1, ny):
            keys = keys + shift(keys_parts[d], "y", d)
        keys = keys.astype(BF16)
    with jax.named_scope("sums_over_adapter"):
        sums = slot_sums(slots, terms, slot_count)
        owned = lax.all_to_all(sums, ADAPTER, split_axis=0, concat_axis=0, tiled=True)
    grad_down, grad_up = finish(owned.reshape((nx, nq, npair) + owned.shape[1:]), part)
    return (keys, grad_down.reshape(1, width, rank), grad_up.reshape(1, rank, features))


def solution(mesh):
    chips = Mesh(mesh.devices.reshape(4, 4, 2, 4, 2), ("x", "zq", "zp", "y", "core"))
    return jax.shard_map(
        per_device,
        mesh=chips,
        in_specs=(
            P(ADAPTER, SEQ),
            P(SEQ, None),
            P(ADAPTER + SEQ, None),
            P(ADAPTER, SEQ),
            P(None, None, SEQ),
            P(ADAPTER, None),
            P(ADAPTER),
            P(),
        ),
        out_specs=(
            P(ADAPTER + SEQ, None),
            P(ADAPTER, SEQ, None),
            P(ADAPTER, None, SEQ),
        ),
        check_vma=False,
    )
```

```python
import jax
import jax.numpy as jnp
from jax import lax
from jax.experimental import pallas as pl
from jax.experimental.pallas import tpu as pltpu
from jax.sharding import Mesh, PartitionSpec as P

BLK = 128
ADAPTER_SCALE = 2.0
SEQ = ("y", "core")
FIRST = ("x", "zp")
ADAPTER = ("x", "zq", "zp")
SLOT_ROWS = 16
LIMIT = pltpu.CompilerParams(vmem_limit_bytes=16 * 1024 * 1024)
WHOLE = pltpu.CompilerParams(vmem_limit_bytes=60 * 1024 * 1024)
VMEM = pl.BlockSpec(memory_space=pltpu.VMEM)
SMEM = pl.BlockSpec(memory_space=pltpu.SMEM)
HBM = pl.BlockSpec(memory_space=pltpu.HBM)
BF16 = jnp.bfloat16
F32 = jnp.float32


def shift(value, axis, distance):
    size = lax.axis_size(axis)
    return lax.ppermute(value, axis, [(i, (i + distance) % size) for i in range(size)])


def contract(left, right, left_dim, right_dim):
    return lax.dot_general(
        left, right, (((left_dim,), (right_dim,)), ((), ())), preferred_element_type=F32
    )


def masked(cot_ref, fill_ref, b):
    block = cot_ref[b * BLK : (b + 1) * BLK, :]
    position = lax.broadcasted_iota(jnp.int32, block.shape, 0)
    return jnp.where(position < fill_ref[b], block, jnp.zeros_like(block))


def mid_partials(jobs, fills, up_stack, cotangent, saved):
    nblocks = jobs.shape[0]
    rank, features = up_stack.shape[1:]
    half = nblocks // 2

    def kernel(
        jobs_ref, fill_ref, up_ref, cot_ref, saved_ref, own_ref, other_ref, picked_ref, cot, sems
    ):
        copies = []
        for b in range(nblocks):
            block = slice(b * BLK, (b + 1) * BLK)
            pair = (
                pltpu.make_async_copy(up_ref.at[jobs_ref[b]], picked_ref.at[b], sems.at[2 * b]),
                pltpu.make_async_copy(cot_ref.at[block, :], cot.at[block, :], sems.at[2 * b + 1]),
            )
            for copy in pair:
                copy.start()
            copies.append(pair)
        core = lax.axis_index("core")
        own_ref[half] = saved_ref[...].astype(F32)
        other_ref[half] = saved_ref[...].astype(F32)
        for i in range(half):
            partials = []
            for b in (2 * i, 2 * i + 1):
                for copy in copies[b]:
                    copy.wait()
                partials.append(contract(masked(cot, fill_ref, b), picked_ref[b], 1, 1))
            own_ref[i] = jnp.where(core == 0, partials[0], partials[1])
            other_ref[i] = jnp.where(core == 0, partials[1], partials[0])

    out = jax.ShapeDtypeStruct((half + 1, BLK, rank), F32)
    return pl.pallas_call(
        kernel,
        out_shape=[out, out, jax.ShapeDtypeStruct((nblocks, rank, features), BF16)],
        in_specs=[SMEM, SMEM, HBM, HBM, VMEM],
        out_specs=[VMEM] * 3,
        scratch_shapes=[
            pltpu.VMEM(cotangent.shape, BF16),
            pltpu.SemaphoreType.DMA((2 * nblocks,)),
        ],
        compiler_params=WHOLE,
        name="mid_partials",
    )(jobs, fills, up_stack, cotangent, saved)


def y_payload(own, received):
    half, _, rank = own.shape
    half -= 1

    def kernel(own_ref, received_ref, keep_ref, out_ref):
        first = lax.axis_index("core") == 0
        mine, theirs = own_ref[half], received_ref[half]
        out_ref[2 * half] = jnp.where(first, mine, theirs).astype(BF16)
        out_ref[2 * half + 1] = jnp.where(first, theirs, mine).astype(BF16)
        total = own_ref[:half] + received_ref[:half]
        keep_ref[...] = total
        high = total.astype(BF16)
        out_ref[:half] = high
        out_ref[half : 2 * half] = (total - high.astype(F32)).astype(BF16)

    return pl.pallas_call(
        kernel,
        out_shape=[
            jax.ShapeDtypeStruct((half, BLK, rank), F32),
            jax.ShapeDtypeStruct((2 * half + 2, BLK, rank), BF16),
        ],
        in_specs=[VMEM] * 2,
        out_specs=[VMEM] * 2,
        compiler_params=LIMIT,
        name="y_payload",
    )(own, received)


def mid_grads(keep, sent, received):
    half, _, rank = keep.shape
    ny = len(received) + 1

    def kernel(keep_ref, sent_ref, *refs):
        got = refs[: ny - 1]
        mids_ref, rows_ref = refs[ny - 1 :]
        y = lax.axis_index("y")
        total = keep_ref[...]
        for ref in got:
            total += ref[:half].astype(F32) + ref[half : 2 * half].astype(F32)
        mids_ref[...] = total.astype(BF16)
        for d, ref in enumerate((sent_ref,) + got):
            source = lax.rem(y + ny - d, ny)
            rows_ref[2 * source] = ref[2 * half]
            rows_ref[2 * source + 1] = ref[2 * half + 1]

    return pl.pallas_call(
        kernel,
        out_shape=[
            jax.ShapeDtypeStruct((half, BLK, rank), BF16),
            jax.ShapeDtypeStruct((2 * half, BLK, rank), BF16),
        ],
        in_specs=[VMEM] * (ny + 1),
        out_specs=[VMEM] * 2,
        compiler_params=LIMIT,
        name="mid_grads",
    )(keep, sent, *received)


def products(jobs, fills, slot_of, tokens, mids, mids_other, saved_rows, cotangent, parts):
    width = tokens.shape[1]
    nblocks, _, rank = saved_rows.shape
    part, split = width // parts, rank // parts
    height = part + split

    def kernel(
        jobs_ref, fill_ref, slot_ref, tokens_ref, mids_ref, other_ref, saved_ref, cot_ref, out_ref
    ):
        core = lax.axis_index("core")
        row = lax.broadcasted_iota(jnp.int32, (SLOT_ROWS, rank), 0)
        slots = jnp.zeros((SLOT_ROWS, rank), jnp.int32)
        for b in range(nblocks):
            slots = jnp.where(row == b, slot_ref[jobs_ref[b]], slots)
        slots = slots.astype(F32).astype(BF16)
        for i in range(parts):
            out_ref[i, nblocks * height :, :] = slots
        for b in range(nblocks):
            mine, other = mids_ref[b // 2], other_ref[b // 2]
            mid = jnp.where(core == b % 2, mine, other)
            up = contract(saved_ref[b], masked(cot_ref, fill_ref, b), 0, 0).astype(BF16)
            first = b * height
            for i in range(parts):
                block = tokens_ref[b * BLK : (b + 1) * BLK, i * part : (i + 1) * part]
                out_ref[i, first : first + part, :] = contract(block, mid, 0, 0).astype(BF16)
                out_ref[i, first + part : first + height, :] = up[i * split : (i + 1) * split]

    return pl.pallas_call(
        kernel,
        out_shape=jax.ShapeDtypeStruct((parts, nblocks * height + SLOT_ROWS, rank), BF16),
        in_specs=[SMEM] * 3 + [VMEM] * 5,
        out_specs=VMEM,
        compiler_params=LIMIT,
        name="products",
    )(jobs, fills, slot_of, tokens, mids, mids_other, saved_rows, cotangent)


def slot_sums(slots, terms, slot_count):
    groups, nblocks = slots.shape
    rank = terms.shape[2]
    height = (terms.shape[1] - SLOT_ROWS) // nblocks

    def kernel(slots_ref, terms_ref, out_ref, acc):
        acc[...] = jnp.zeros_like(acc)
        for g in range(groups):
            for b in range(nblocks):
                acc[slots_ref[g, b]] += terms_ref[g, b * height : (b + 1) * height, :].astype(F32)
        out_ref[...] = acc[...].astype(BF16)

    return pl.pallas_call(
        kernel,
        out_shape=jax.ShapeDtypeStruct((slot_count, height, rank), BF16),
        in_specs=[SMEM, VMEM],
        out_specs=VMEM,
        scratch_shapes=[pltpu.VMEM((slot_count, height, rank), F32)],
        compiler_params=LIMIT,
        name="slot_sums",
    )(slots, terms)


def finish(owned, part):
    nx, nq, npair, height, rank = owned.shape
    parts, split = nx * npair, height - part

    def kernel(owned_ref, down_ref, up_ref):
        for x in range(nx):
            for p in range(npair):
                total = owned_ref[x, 0, p].astype(F32)
                for q in range(1, nq):
                    total += owned_ref[x, q, p].astype(F32)
                total = ADAPTER_SCALE * total
                down_ref[x * npair + p] = total[:part]
                up_ref[x * npair + p] = total[part:]

    return pl.pallas_call(
        kernel,
        out_shape=[
            jax.ShapeDtypeStruct((parts, part, rank), F32),
            jax.ShapeDtypeStruct((parts, split, rank), F32),
        ],
        in_specs=[VMEM],
        out_specs=[VMEM, VMEM],
        compiler_params=LIMIT,
        name="finish",
    )(owned)


def keys_partials(place, tokens, frozen_weight, saved_rows, picked):
    rows, width = tokens.shape
    nblocks, rank, features = picked.shape
    half = nblocks // 2
    total = frozen_weight.shape[1]

    def block_of(i, j, place_ref):
        return 2 * j + lax.rem(place_ref[1] + i, 2)

    def kernel(place_ref, tokens_ref, weight_ref, saved_ref, picked_ref, own_ref, other_ref):
        columns = pl.ds(pl.multiple_of((2 * place_ref[0] + place_ref[1]) * features, features), features)
        for i, out_ref in enumerate((own_ref, other_ref)):

            @pl.when(pl.program_id(0) == i)
            def _():
                out_ref[0] = jnp.dot(tokens_ref[...], weight_ref[...], preferred_element_type=F32)
                out_ref[0, :, columns] += ADAPTER_SCALE * jnp.dot(
                    saved_ref[0], picked_ref[0], preferred_element_type=F32
                )

    shape = jax.ShapeDtypeStruct((half, BLK, total), F32)
    return pl.pallas_call(
        kernel,
        grid_spec=pltpu.PrefetchScalarGridSpec(
            num_scalar_prefetch=1,
            grid=(2, half),
            in_specs=[
                pl.BlockSpec((BLK, width), lambda i, j, place: (block_of(i, j, place), 0)),
                pl.BlockSpec((width, total), lambda i, j, place: (0, 0)),
                pl.BlockSpec((1, BLK, rank), lambda i, j, place: (block_of(i, j, place), 0, 0)),
                pl.BlockSpec((1, rank, features), lambda i, j, place: (block_of(i, j, place), 0, 0)),
            ],
            out_specs=[
                pl.BlockSpec((1, BLK, total), lambda i, j, place: (jnp.where(i == 0, j, half - 1), 0, 0)),
                pl.BlockSpec((1, BLK, total), lambda i, j, place: (jnp.where(i == 0, 0, j), 0, 0)),
            ],
        ),
        out_shape=[shape, shape],
        compiler_params=LIMIT,
        name="keys_partials",
    )(place, tokens, frozen_weight, saved_rows, picked)


def keys_chip_sums(own, received):
    ny, block, total = own.shape

    def kernel(own_ref, received_ref, *outs):
        for d in range(ny):
            to = lax.rem(lax.axis_index("y") + d, ny)
            outs[d][...] = own_ref[to] + received_ref[to]

    return pl.pallas_call(
        kernel,
        out_shape=[jax.ShapeDtypeStruct((block, total), F32)] * ny,
        in_specs=[VMEM, VMEM],
        out_specs=[VMEM] * ny,
        compiler_params=LIMIT,
        name="keys_chip_sums",
    )(own, received)


def per_device(
    tokens, frozen_weight, saved_mid, cotangent, up_stack, block_job, block_fill, slot_of
):
    width = tokens.shape[1]
    features = cotangent.shape[1]
    rank = saved_mid.shape[1]
    nblocks = block_job.shape[0]
    slot_count = slot_of.shape[0]
    nx, nq, npair, ny = (lax.axis_size(name) for name in ADAPTER + ("y",))
    parts = nx * npair
    part, split = width // parts, rank // parts
    jobs = block_job.reshape(nblocks)
    place = jnp.stack([lax.axis_index(name) for name in SEQ]).astype(jnp.int32)

    with jax.named_scope("mid_sums"):
        own, other, picked = mid_partials(jobs, block_fill, up_stack, cotangent, saved_mid)
        keep, sent = y_payload(own, shift(other, "core", 1))
        received = [shift(sent, "y", d) for d in range(1, ny)]
        mids, saved_rows = mid_grads(keep, sent, received)
        mids_other = shift(mids, "core", 1)
    with jax.named_scope("terms_over_first"):
        terms = products(
            jobs, block_fill, slot_of, tokens, mids, mids_other, saved_rows, cotangent, parts
        )
        terms = lax.all_to_all(terms, FIRST, split_axis=0, concat_axis=0, tiled=True)
    with jax.named_scope("keys_core"):
        keys_own, keys_other = keys_partials(place, tokens, frozen_weight, saved_rows, picked)
        keys_parts = keys_chip_sums(keys_own, shift(keys_other, "core", 1))
        terms, keys_parts = lax.optimization_barrier((terms, keys_parts))
    with jax.named_scope("keys_y"):
        keys = keys_parts[0]
        for d in range(1, ny):
            keys = keys + shift(keys_parts[d], "y", d)
        keys = keys.astype(BF16)
    with jax.named_scope("sums_over_adapter"):
        tail = nblocks * (part + split)
        slots = terms[:, tail : tail + nblocks, 0].astype(jnp.int32)
        sums = slot_sums(slots, terms, slot_count)
        owned = lax.all_to_all(sums, ADAPTER, split_axis=0, concat_axis=0, tiled=True)
    grad_down, grad_up = finish(owned.reshape((nx, nq, npair) + owned.shape[1:]), part)
    return (keys, grad_down.reshape(1, width, rank), grad_up.reshape(1, rank, features))


def solution(mesh):
    chips = Mesh(mesh.devices.reshape(4, 4, 2, 4, 2), ("x", "zq", "zp", "y", "core"))
    return jax.shard_map(
        per_device,
        mesh=chips,
        in_specs=(
            P(ADAPTER, SEQ),
            P(SEQ, None),
            P(ADAPTER + SEQ, None),
            P(ADAPTER, SEQ),
            P(None, None, SEQ),
            P(ADAPTER, None),
            P(ADAPTER),
            P(),
        ),
        out_specs=(
            P(ADAPTER + SEQ, None),
            P(ADAPTER, SEQ, None),
            P(ADAPTER, None, SEQ),
        ),
        check_vma=False,
    )
```

```python
import jax
import jax.numpy as jnp
from jax import lax
from jax.experimental import pallas as pl
from jax.experimental.pallas import tpu as pltpu
from jax.sharding import Mesh, PartitionSpec as P

BLK = 128
ADAPTER_SCALE = 2.0
SEQ = ("y", "core")
FIRST = ("x", "zp")
ADAPTER = ("x", "zq", "zp")
SLOT_ROWS = 16
LIMIT = pltpu.CompilerParams(vmem_limit_bytes=16 * 1024 * 1024)
WHOLE = pltpu.CompilerParams(vmem_limit_bytes=60 * 1024 * 1024)
VMEM = pl.BlockSpec(memory_space=pltpu.VMEM)
SMEM = pl.BlockSpec(memory_space=pltpu.SMEM)
HBM = pl.BlockSpec(memory_space=pltpu.HBM)
BF16 = jnp.bfloat16
F32 = jnp.float32


def shift(value, axis, distance):
    size = lax.axis_size(axis)
    return lax.ppermute(value, axis, [(i, (i + distance) % size) for i in range(size)])


def contract(left, right, left_dim, right_dim):
    return lax.dot_general(
        left, right, (((left_dim,), (right_dim,)), ((), ())), preferred_element_type=F32
    )


def masked(cot_ref, fill_ref, b):
    block = cot_ref[b * BLK : (b + 1) * BLK, :]
    position = lax.broadcasted_iota(jnp.int32, block.shape, 0)
    return jnp.where(position < fill_ref[b], block, jnp.zeros_like(block))


def mid_partials(jobs, fills, up_stack, cotangent, saved):
    nblocks = jobs.shape[0]
    rank, features = up_stack.shape[1:]
    half = nblocks // 2

    def kernel(
        jobs_ref, fill_ref, up_ref, cot_ref, saved_ref, own_ref, other_ref, picked_ref, cot, sems
    ):
        copies = []
        for b in range(nblocks):
            block = slice(b * BLK, (b + 1) * BLK)
            pair = (
                pltpu.make_async_copy(up_ref.at[jobs_ref[b]], picked_ref.at[b], sems.at[2 * b]),
                pltpu.make_async_copy(cot_ref.at[block, :], cot.at[block, :], sems.at[2 * b + 1]),
            )
            for copy in pair:
                copy.start()
            copies.append(pair)
        core = lax.axis_index("core")
        own_ref[half] = saved_ref[...].astype(F32)
        other_ref[half] = saved_ref[...].astype(F32)
        for i in range(half):
            partials = []
            for b in (2 * i, 2 * i + 1):
                for copy in copies[b]:
                    copy.wait()
                partials.append(contract(masked(cot, fill_ref, b), picked_ref[b], 1, 1))
            own_ref[i] = jnp.where(core == 0, partials[0], partials[1])
            other_ref[i] = jnp.where(core == 0, partials[1], partials[0])

    out = jax.ShapeDtypeStruct((half + 1, BLK, rank), F32)
    return pl.pallas_call(
        kernel,
        out_shape=[out, out, jax.ShapeDtypeStruct((nblocks, rank, features), BF16)],
        in_specs=[SMEM, SMEM, HBM, HBM, VMEM],
        out_specs=[VMEM] * 3,
        scratch_shapes=[
            pltpu.VMEM(cotangent.shape, BF16),
            pltpu.SemaphoreType.DMA((2 * nblocks,)),
        ],
        compiler_params=WHOLE,
        name="mid_partials",
    )(jobs, fills, up_stack, cotangent, saved)


def halves_of(total):
    high = total.astype(BF16)
    return high, (total - high.astype(F32)).astype(BF16)


def y_first(own, received):
    half, _, rank = own.shape
    half -= 1
    each = half // 2

    def kernel(own_ref, received_ref, keep_ref, *outs):
        first = lax.axis_index("core") == 0
        mine, theirs = own_ref[half], received_ref[half]
        total = own_ref[:half] + received_ref[:half]
        keep_ref[...] = total
        for i, out in enumerate(outs):
            out[:each], out[each : 2 * each] = halves_of(total[i * each : (i + 1) * each])
            saved = jnp.where(first, mine, theirs) if i == 0 else jnp.where(first, theirs, mine)
            out[2 * each] = saved.astype(BF16)

    return pl.pallas_call(
        kernel,
        out_shape=[jax.ShapeDtypeStruct((half, BLK, rank), F32)]
        + [jax.ShapeDtypeStruct((2 * each + 1, BLK, rank), BF16)] * 2,
        in_specs=[VMEM] * 2,
        out_specs=[VMEM] * 3,
        compiler_params=LIMIT,
        name="y_first",
    )(own, received)


def y_second(keep, sent, received):
    half, _, rank = keep.shape
    each = half // 2

    def kernel(keep_ref, *refs):
        sent_refs, got_refs, total_ref, outs = refs[:2], refs[2:4], refs[4], refs[5:]
        for i in range(2):
            got = got_refs[i]
            blocks = slice(i * each, (i + 1) * each)
            total = keep_ref[blocks] + got[:each].astype(F32) + got[each : 2 * each].astype(F32)
            total_ref[blocks] = total
            outs[i][:each], outs[i][each : 2 * each] = halves_of(total)
            outs[i][2 * each] = sent_refs[i][2 * each]
            outs[i][2 * each + 1] = got[2 * each]

    return pl.pallas_call(
        kernel,
        out_shape=[jax.ShapeDtypeStruct(keep.shape, F32)]
        + [jax.ShapeDtypeStruct((2 * each + 2, BLK, rank), BF16)] * 2,
        in_specs=[VMEM] * 5,
        out_specs=[VMEM] * 3,
        compiler_params=LIMIT,
        name="y_second",
    )(keep, *sent, *received)


def mid_grads(total, sent, received):
    half, _, rank = total.shape
    each = half // 2

    def kernel(total_ref, *refs):
        sent_refs, got_refs, mids_ref, rows_ref = refs[:2], refs[2:4], refs[4], refs[5]
        y = lax.axis_index("y")
        pair, mirror = lax.bitwise_xor(y, 1), half - 1 - y
        for i, (near, far) in enumerate(((pair, mirror), (mirror, pair))):
            got = got_refs[i]
            blocks = slice(i * each, (i + 1) * each)
            mids_ref[blocks] = (
                total_ref[blocks] + got[:each].astype(F32) + got[each : 2 * each].astype(F32)
            ).astype(BF16)
            beyond = lax.bitwise_xor(far, 1) if i == 0 else half - 1 - far
            rows_ref[2 * y + i] = sent_refs[i][2 * each]
            rows_ref[2 * near + i] = sent_refs[i][2 * each + 1]
            rows_ref[2 * far + i] = got[2 * each]
            rows_ref[2 * beyond + i] = got[2 * each + 1]

    return pl.pallas_call(
        kernel,
        out_shape=[
            jax.ShapeDtypeStruct((half, BLK, rank), BF16),
            jax.ShapeDtypeStruct((2 * half, BLK, rank), BF16),
        ],
        in_specs=[VMEM] * 5,
        out_specs=[VMEM] * 2,
        compiler_params=LIMIT,
        name="mid_grads",
    )(total, *sent, *received)


def products(jobs, fills, slot_of, tokens, mids, mids_other, saved_rows, cotangent, parts):
    width = tokens.shape[1]
    nblocks, _, rank = saved_rows.shape
    part, split = width // parts, rank // parts
    height = part + split

    def kernel(
        jobs_ref, fill_ref, slot_ref, tokens_ref, mids_ref, other_ref, saved_ref, cot_ref, out_ref
    ):
        core = lax.axis_index("core")
        row = lax.broadcasted_iota(jnp.int32, (SLOT_ROWS, rank), 0)
        slots = jnp.zeros((SLOT_ROWS, rank), jnp.int32)
        for b in range(nblocks):
            slots = jnp.where(row == b, slot_ref[jobs_ref[b]], slots)
        slots = slots.astype(F32).astype(BF16)
        for i in range(parts):
            out_ref[i, nblocks * height :, :] = slots
        for b in range(nblocks):
            mine, other = mids_ref[b // 2], other_ref[b // 2]
            mid = jnp.where(core == b % 2, mine, other)
            up = contract(saved_ref[b], masked(cot_ref, fill_ref, b), 0, 0).astype(BF16)
            first = b * height
            for i in range(parts):
                block = tokens_ref[b * BLK : (b + 1) * BLK, i * part : (i + 1) * part]
                out_ref[i, first : first + part, :] = contract(block, mid, 0, 0).astype(BF16)
                out_ref[i, first + part : first + height, :] = up[i * split : (i + 1) * split]

    return pl.pallas_call(
        kernel,
        out_shape=jax.ShapeDtypeStruct((parts, nblocks * height + SLOT_ROWS, rank), BF16),
        in_specs=[SMEM] * 3 + [VMEM] * 5,
        out_specs=VMEM,
        compiler_params=LIMIT,
        name="products",
    )(jobs, fills, slot_of, tokens, mids, mids_other, saved_rows, cotangent)


def slot_sums(slots, terms, slot_count):
    groups, nblocks = slots.shape
    rank = terms.shape[2]
    height = (terms.shape[1] - SLOT_ROWS) // nblocks

    def kernel(slots_ref, terms_ref, out_ref, acc):
        acc[...] = jnp.zeros_like(acc)
        for g in range(groups):
            for b in range(nblocks):
                acc[slots_ref[g, b]] += terms_ref[g, b * height : (b + 1) * height, :].astype(F32)
        out_ref[...] = acc[...].astype(BF16)

    return pl.pallas_call(
        kernel,
        out_shape=jax.ShapeDtypeStruct((slot_count, height, rank), BF16),
        in_specs=[SMEM, VMEM],
        out_specs=VMEM,
        scratch_shapes=[pltpu.VMEM((slot_count, height, rank), F32)],
        compiler_params=LIMIT,
        name="slot_sums",
    )(slots, terms)


def finish(owned, part):
    nx, nq, npair, height, rank = owned.shape
    parts, split = nx * npair, height - part

    def kernel(owned_ref, down_ref, up_ref):
        for x in range(nx):
            for p in range(npair):
                total = owned_ref[x, 0, p].astype(F32)
                for q in range(1, nq):
                    total += owned_ref[x, q, p].astype(F32)
                total = ADAPTER_SCALE * total
                down_ref[x * npair + p] = total[:part]
                up_ref[x * npair + p] = total[part:]

    return pl.pallas_call(
        kernel,
        out_shape=[
            jax.ShapeDtypeStruct((parts, part, rank), F32),
            jax.ShapeDtypeStruct((parts, split, rank), F32),
        ],
        in_specs=[VMEM],
        out_specs=[VMEM, VMEM],
        compiler_params=LIMIT,
        name="finish",
    )(owned)


def keys_partials(place, tokens, frozen_weight, saved_rows, picked):
    rows, width = tokens.shape
    nblocks, rank, features = picked.shape
    half = nblocks // 2
    total = frozen_weight.shape[1]

    def block_of(i, j, place_ref):
        return 2 * j + lax.rem(place_ref[1] + i, 2)

    def kernel(place_ref, tokens_ref, weight_ref, saved_ref, picked_ref, own_ref, other_ref):
        columns = pl.ds(pl.multiple_of((2 * place_ref[0] + place_ref[1]) * features, features), features)
        for i, out_ref in enumerate((own_ref, other_ref)):

            @pl.when(pl.program_id(0) == i)
            def _():
                out_ref[0] = jnp.dot(tokens_ref[...], weight_ref[...], preferred_element_type=F32)
                out_ref[0, :, columns] += ADAPTER_SCALE * jnp.dot(
                    saved_ref[0], picked_ref[0], preferred_element_type=F32
                )

    shape = jax.ShapeDtypeStruct((half, BLK, total), F32)
    return pl.pallas_call(
        kernel,
        grid_spec=pltpu.PrefetchScalarGridSpec(
            num_scalar_prefetch=1,
            grid=(2, half),
            in_specs=[
                pl.BlockSpec((BLK, width), lambda i, j, place: (block_of(i, j, place), 0)),
                pl.BlockSpec((width, total), lambda i, j, place: (0, 0)),
                pl.BlockSpec((1, BLK, rank), lambda i, j, place: (block_of(i, j, place), 0, 0)),
                pl.BlockSpec((1, rank, features), lambda i, j, place: (block_of(i, j, place), 0, 0)),
            ],
            out_specs=[
                pl.BlockSpec((1, BLK, total), lambda i, j, place: (jnp.where(i == 0, j, half - 1), 0, 0)),
                pl.BlockSpec((1, BLK, total), lambda i, j, place: (jnp.where(i == 0, 0, j), 0, 0)),
            ],
        ),
        out_shape=[shape, shape],
        compiler_params=LIMIT,
        name="keys_partials",
    )(place, tokens, frozen_weight, saved_rows, picked)


def keys_chip_sums(own, received):
    ny, block, total = own.shape

    def kernel(own_ref, received_ref, *outs):
        for d in range(ny):
            to = lax.rem(lax.axis_index("y") + d, ny)
            outs[d][...] = own_ref[to] + received_ref[to]

    return pl.pallas_call(
        kernel,
        out_shape=[jax.ShapeDtypeStruct((block, total), F32)] * ny,
        in_specs=[VMEM, VMEM],
        out_specs=[VMEM] * ny,
        compiler_params=LIMIT,
        name="keys_chip_sums",
    )(own, received)


def per_device(
    tokens, frozen_weight, saved_mid, cotangent, up_stack, block_job, block_fill, slot_of
):
    width = tokens.shape[1]
    features = cotangent.shape[1]
    rank = saved_mid.shape[1]
    nblocks = block_job.shape[0]
    slot_count = slot_of.shape[0]
    nx, nq, npair, ny = (lax.axis_size(name) for name in ADAPTER + ("y",))
    parts = nx * npair
    part, split = width // parts, rank // parts
    jobs = block_job.reshape(nblocks)
    place = jnp.stack([lax.axis_index(name) for name in SEQ]).astype(jnp.int32)

    with jax.named_scope("mid_sums"):
        own, other, picked = mid_partials(jobs, block_fill, up_stack, cotangent, saved_mid)
        keep, *sent = y_first(own, shift(other, "core", 1))
        pair = [(i, i ^ 1) for i in range(ny)]
        mirror = [(i, ny - 1 - i) for i in range(ny)]
        received = [lax.ppermute(sent[0], "y", pair), lax.ppermute(sent[1], "y", mirror)]
        total, *sent = y_second(keep, sent, received)
        received = [lax.ppermute(sent[0], "y", mirror), lax.ppermute(sent[1], "y", pair)]
        mids, saved_rows = mid_grads(total, sent, received)
        mids_other = shift(mids, "core", 1)
    with jax.named_scope("terms_over_first"):
        terms = products(
            jobs, block_fill, slot_of, tokens, mids, mids_other, saved_rows, cotangent, parts
        )
        terms = lax.all_to_all(terms, FIRST, split_axis=0, concat_axis=0, tiled=True)
    with jax.named_scope("keys_core"):
        keys_own, keys_other = keys_partials(place, tokens, frozen_weight, saved_rows, picked)
        keys_parts = keys_chip_sums(keys_own, shift(keys_other, "core", 1))
        terms, keys_parts = lax.optimization_barrier((terms, keys_parts))
    with jax.named_scope("keys_y"):
        keys = keys_parts[0]
        for d in range(1, ny):
            keys = keys + shift(keys_parts[d], "y", d)
        keys = keys.astype(BF16)
    with jax.named_scope("sums_over_adapter"):
        tail = nblocks * (part + split)
        slots = terms[:, tail : tail + nblocks, 0].astype(jnp.int32)
        sums = slot_sums(slots, terms, slot_count)
        owned = lax.all_to_all(sums, ADAPTER, split_axis=0, concat_axis=0, tiled=True)
    grad_down, grad_up = finish(owned.reshape((nx, nq, npair) + owned.shape[1:]), part)
    return (keys, grad_down.reshape(1, width, rank), grad_up.reshape(1, rank, features))


def solution(mesh):
    chips = Mesh(mesh.devices.reshape(4, 4, 2, 4, 2), ("x", "zq", "zp", "y", "core"))
    return jax.shard_map(
        per_device,
        mesh=chips,
        in_specs=(
            P(ADAPTER, SEQ),
            P(SEQ, None),
            P(ADAPTER + SEQ, None),
            P(ADAPTER, SEQ),
            P(None, None, SEQ),
            P(ADAPTER, None),
            P(ADAPTER),
            P(),
        ),
        out_specs=(
            P(ADAPTER + SEQ, None),
            P(ADAPTER, SEQ, None),
            P(ADAPTER, None, SEQ),
        ),
        check_vma=False,
    )
```

```python
import jax
import jax.numpy as jnp
from jax import lax
from jax.experimental import pallas as pl
from jax.experimental.pallas import tpu as pltpu
from jax.sharding import Mesh, PartitionSpec as P

BLK = 128
ADAPTER_SCALE = 2.0
SEQ = ("y", "core")
FIRST = ("x", "zp")
ADAPTER = ("x", "zq", "zp")
SLOT_ROWS = 16
LIMIT = pltpu.CompilerParams(vmem_limit_bytes=16 * 1024 * 1024)
WHOLE = pltpu.CompilerParams(vmem_limit_bytes=60 * 1024 * 1024)
VMEM = pl.BlockSpec(memory_space=pltpu.VMEM)
SMEM = pl.BlockSpec(memory_space=pltpu.SMEM)
HBM = pl.BlockSpec(memory_space=pltpu.HBM)
BF16 = jnp.bfloat16
F32 = jnp.float32


def shift(value, axis, distance):
    size = lax.axis_size(axis)
    return lax.ppermute(value, axis, [(i, (i + distance) % size) for i in range(size)])


def contract(left, right, left_dim, right_dim):
    return lax.dot_general(
        left, right, (((left_dim,), (right_dim,)), ((), ())), preferred_element_type=F32
    )


def masked(cot_ref, fill_ref, b):
    block = cot_ref[b * BLK : (b + 1) * BLK, :]
    position = lax.broadcasted_iota(jnp.int32, block.shape, 0)
    return jnp.where(position < fill_ref[b], block, jnp.zeros_like(block))


def mid_partials(jobs, fills, up_stack, cotangent, saved):
    nblocks = jobs.shape[0]
    rank, features = up_stack.shape[1:]
    half = nblocks // 2

    def kernel(
        jobs_ref, fill_ref, up_ref, cot_ref, saved_ref, own_ref, other_ref, picked_ref, cot, sems
    ):
        whole = pltpu.make_async_copy(cot_ref, cot, sems.at[nblocks])
        whole.start()
        copies = [
            pltpu.make_async_copy(up_ref.at[jobs_ref[b]], picked_ref.at[b], sems.at[b])
            for b in range(nblocks)
        ]
        for copy in copies:
            copy.start()
        core = lax.axis_index("core")
        own_ref[half] = saved_ref[...].astype(F32)
        other_ref[half] = saved_ref[...].astype(F32)
        whole.wait()
        for copy in copies:
            copy.wait()
        for i in range(half):
            partials = []
            for b in (2 * i, 2 * i + 1):
                partials.append(contract(masked(cot, fill_ref, b), picked_ref[b], 1, 1))
            own_ref[i] = jnp.where(core == 0, partials[0], partials[1])
            other_ref[i] = jnp.where(core == 0, partials[1], partials[0])

    out = jax.ShapeDtypeStruct((half + 1, BLK, rank), F32)
    return pl.pallas_call(
        kernel,
        out_shape=[out, out],
        in_specs=[SMEM, SMEM, HBM, HBM, VMEM],
        out_specs=[VMEM] * 2,
        scratch_shapes=[
            pltpu.VMEM((nblocks, rank, features), BF16),
            pltpu.VMEM(cotangent.shape, BF16),
            pltpu.SemaphoreType.DMA((nblocks + 1,)),
        ],
        compiler_params=WHOLE,
        name="mid_partials",
    )(jobs, fills, up_stack, cotangent, saved)


def halves_of(total):
    high = total.astype(BF16)
    return high, (total - high.astype(F32)).astype(BF16)


def own_parts(own):
    half, _, rank = own.shape
    half -= 1

    def kernel(own_ref, sums_ref, saved_ref):
        sums_ref[...] = own_ref[:half]
        saved_ref[...] = own_ref[half].astype(BF16)

    return pl.pallas_call(
        kernel,
        out_shape=[
            jax.ShapeDtypeStruct((half, BLK, rank), F32),
            jax.ShapeDtypeStruct((BLK, rank), BF16),
        ],
        in_specs=[VMEM],
        out_specs=[VMEM] * 2,
        compiler_params=LIMIT,
        name="own_parts",
    )(own)


def y_first(own, saved, received):
    half, _, rank = own.shape
    each = half // 2

    def kernel(own_ref, saved_ref, received_ref, keep_ref, *outs):
        first = lax.axis_index("core") == 0
        mine, theirs = saved_ref[...], received_ref[half].astype(BF16)
        total = own_ref[...] + received_ref[:half]
        keep_ref[...] = total
        for i, out in enumerate(outs):
            out[:each], out[each : 2 * each] = halves_of(total[i * each : (i + 1) * each])
            out[2 * each] = jnp.where(first, *((mine, theirs) if i == 0 else (theirs, mine)))

    return pl.pallas_call(
        kernel,
        out_shape=[jax.ShapeDtypeStruct((half, BLK, rank), F32)]
        + [jax.ShapeDtypeStruct((2 * each + 1, BLK, rank), BF16)] * 2,
        in_specs=[VMEM] * 3,
        out_specs=[VMEM] * 3,
        compiler_params=LIMIT,
        name="y_first",
    )(own, saved, received)


def y_second(keep, sent, received):
    half, _, rank = keep.shape
    each = half // 2

    def kernel(keep_ref, *refs):
        sent_refs, got_refs, total_ref, outs = refs[:2], refs[2:4], refs[4], refs[5:]
        for i in range(2):
            got = got_refs[i]
            blocks = slice(i * each, (i + 1) * each)
            total = keep_ref[blocks] + got[:each].astype(F32) + got[each : 2 * each].astype(F32)
            total_ref[blocks] = total
            outs[i][:each], outs[i][each : 2 * each] = halves_of(total)
            outs[i][2 * each] = sent_refs[i][2 * each]
            outs[i][2 * each + 1] = got[2 * each]

    return pl.pallas_call(
        kernel,
        out_shape=[jax.ShapeDtypeStruct(keep.shape, F32)]
        + [jax.ShapeDtypeStruct((2 * each + 2, BLK, rank), BF16)] * 2,
        in_specs=[VMEM] * 5,
        out_specs=[VMEM] * 3,
        compiler_params=LIMIT,
        name="y_second",
    )(keep, *sent, *received)


def mid_grads(total, sent, received):
    half, _, rank = total.shape
    each = half // 2

    def kernel(total_ref, *refs):
        sent_refs, got_refs, mids_ref, rows_ref = refs[:2], refs[2:4], refs[4], refs[5]
        y = lax.axis_index("y")
        pair, mirror = lax.bitwise_xor(y, 1), half - 1 - y
        for i, (near, far) in enumerate(((pair, mirror), (mirror, pair))):
            got = got_refs[i]
            blocks = slice(i * each, (i + 1) * each)
            mids_ref[blocks] = (
                total_ref[blocks] + got[:each].astype(F32) + got[each : 2 * each].astype(F32)
            ).astype(BF16)
            beyond = lax.bitwise_xor(far, 1) if i == 0 else half - 1 - far
            rows_ref[2 * y + i] = sent_refs[i][2 * each]
            rows_ref[2 * near + i] = sent_refs[i][2 * each + 1]
            rows_ref[2 * far + i] = got[2 * each]
            rows_ref[2 * beyond + i] = got[2 * each + 1]

    return pl.pallas_call(
        kernel,
        out_shape=[
            jax.ShapeDtypeStruct((half, BLK, rank), BF16),
            jax.ShapeDtypeStruct((2 * half, BLK, rank), BF16),
        ],
        in_specs=[VMEM] * 5,
        out_specs=[VMEM] * 2,
        compiler_params=LIMIT,
        name="mid_grads",
    )(total, *sent, *received)


def products(jobs, fills, slot_of, tokens, mids, mids_other, saved_rows, cotangent, parts):
    width = tokens.shape[1]
    nblocks, _, rank = saved_rows.shape
    part, split = width // parts, rank // parts
    height = part + split

    def kernel(
        jobs_ref, fill_ref, slot_ref, tokens_ref, mids_ref, other_ref, saved_ref, cot_ref, out_ref
    ):
        core = lax.axis_index("core")
        row = lax.broadcasted_iota(jnp.int32, (SLOT_ROWS, rank), 0)
        slots = jnp.zeros((SLOT_ROWS, rank), jnp.int32)
        for b in range(nblocks):
            slots = jnp.where(row == b, slot_ref[jobs_ref[b]], slots)
        slots = slots.astype(F32).astype(BF16)
        for i in range(parts):
            out_ref[i, nblocks * height :, :] = slots
        for b in range(nblocks):
            mine, other = mids_ref[b // 2], other_ref[b // 2]
            mid = jnp.where(core == b % 2, mine, other)
            up = contract(saved_ref[b], masked(cot_ref, fill_ref, b), 0, 0).astype(BF16)
            first = b * height
            for i in range(parts):
                block = tokens_ref[b * BLK : (b + 1) * BLK, i * part : (i + 1) * part]
                out_ref[i, first : first + part, :] = contract(block, mid, 0, 0).astype(BF16)
                out_ref[i, first + part : first + height, :] = up[i * split : (i + 1) * split]

    return pl.pallas_call(
        kernel,
        out_shape=jax.ShapeDtypeStruct((parts, nblocks * height + SLOT_ROWS, rank), BF16),
        in_specs=[SMEM] * 3 + [VMEM] * 5,
        out_specs=VMEM,
        compiler_params=LIMIT,
        name="products",
    )(jobs, fills, slot_of, tokens, mids, mids_other, saved_rows, cotangent)


def slot_sums(slots, terms, slot_count):
    groups, nblocks = slots.shape
    rank = terms.shape[2]
    height = (terms.shape[1] - SLOT_ROWS) // nblocks

    def kernel(slots_ref, terms_ref, out_ref, acc):
        acc[...] = jnp.zeros_like(acc)
        for g in range(groups):
            for b in range(nblocks):
                acc[slots_ref[g, b]] += terms_ref[g, b * height : (b + 1) * height, :].astype(F32)
        out_ref[...] = acc[...].astype(BF16)

    return pl.pallas_call(
        kernel,
        out_shape=jax.ShapeDtypeStruct((slot_count, height, rank), BF16),
        in_specs=[SMEM, VMEM],
        out_specs=VMEM,
        scratch_shapes=[pltpu.VMEM((slot_count, height, rank), F32)],
        compiler_params=LIMIT,
        name="slot_sums",
    )(slots, terms)


def finish(owned, part):
    nx, nq, npair, height, rank = owned.shape
    parts, split = nx * npair, height - part

    def kernel(owned_ref, down_ref, up_ref):
        for x in range(nx):
            for p in range(npair):
                total = owned_ref[x, 0, p].astype(F32)
                for q in range(1, nq):
                    total += owned_ref[x, q, p].astype(F32)
                total = ADAPTER_SCALE * total
                down_ref[x * npair + p] = total[:part]
                up_ref[x * npair + p] = total[part:]

    return pl.pallas_call(
        kernel,
        out_shape=[
            jax.ShapeDtypeStruct((parts, part, rank), F32),
            jax.ShapeDtypeStruct((parts, split, rank), F32),
        ],
        in_specs=[VMEM],
        out_specs=[VMEM, VMEM],
        compiler_params=LIMIT,
        name="finish",
    )(owned)


def keys_partials(place, jobs, tokens, frozen_weight, saved_rows, up_stack):
    rows, width = tokens.shape
    nblocks = jobs.shape[0]
    rank, features = up_stack.shape[1:]
    half = nblocks // 2
    total = frozen_weight.shape[1]

    def block_of(i, j, place_ref):
        return 2 * j + lax.rem(place_ref[1] + i, 2)

    def kernel(place_ref, jobs_ref, tokens_ref, weight_ref, saved_ref, picked_ref, own_ref, other_ref):
        columns = pl.ds(pl.multiple_of((2 * place_ref[0] + place_ref[1]) * features, features), features)
        for i, out_ref in enumerate((own_ref, other_ref)):

            @pl.when(pl.program_id(0) == i)
            def _():
                out_ref[0] = jnp.dot(tokens_ref[...], weight_ref[...], preferred_element_type=F32)
                out_ref[0, :, columns] += ADAPTER_SCALE * jnp.dot(
                    saved_ref[0], picked_ref[0], preferred_element_type=F32
                )

    shape = jax.ShapeDtypeStruct((half, BLK, total), F32)
    return pl.pallas_call(
        kernel,
        grid_spec=pltpu.PrefetchScalarGridSpec(
            num_scalar_prefetch=2,
            grid=(2, half),
            in_specs=[
                pl.BlockSpec((BLK, width), lambda i, j, place, jobs: (block_of(i, j, place), 0)),
                pl.BlockSpec((width, total), lambda i, j, place, jobs: (0, 0)),
                pl.BlockSpec((1, BLK, rank), lambda i, j, place, jobs: (block_of(i, j, place), 0, 0)),
                pl.BlockSpec(
                    (1, rank, features),
                    lambda i, j, place, jobs: (jobs[block_of(i, j, place)], 0, 0),
                ),
            ],
            out_specs=[
                pl.BlockSpec((1, BLK, total), lambda i, j, place, jobs: (jnp.where(i == 0, j, half - 1), 0, 0)),
                pl.BlockSpec((1, BLK, total), lambda i, j, place, jobs: (jnp.where(i == 0, 0, j), 0, 0)),
            ],
        ),
        out_shape=[shape, shape],
        compiler_params=LIMIT,
        name="keys_partials",
    )(place, jobs, tokens, frozen_weight, saved_rows, up_stack)


def keys_chip_sums(own, received):
    ny, block, total = own.shape

    def kernel(own_ref, received_ref, *outs):
        for d in range(ny):
            to = lax.rem(lax.axis_index("y") + d, ny)
            outs[d][...] = own_ref[to] + received_ref[to]

    return pl.pallas_call(
        kernel,
        out_shape=[jax.ShapeDtypeStruct((block, total), F32)] * ny,
        in_specs=[VMEM, VMEM],
        out_specs=[VMEM] * ny,
        compiler_params=LIMIT,
        name="keys_chip_sums",
    )(own, received)


def per_device(
    tokens, frozen_weight, saved_mid, cotangent, up_stack, block_job, block_fill, slot_of
):
    width = tokens.shape[1]
    features = cotangent.shape[1]
    rank = saved_mid.shape[1]
    nblocks = block_job.shape[0]
    slot_count = slot_of.shape[0]
    nx, nq, npair, ny = (lax.axis_size(name) for name in ADAPTER + ("y",))
    parts = nx * npair
    part, split = width // parts, rank // parts
    jobs = block_job.reshape(nblocks)
    place = jnp.stack([lax.axis_index(name) for name in SEQ]).astype(jnp.int32)

    with jax.named_scope("mid_sums"):
        own, other = mid_partials(jobs, block_fill, up_stack, cotangent, saved_mid)
        own_sums, own_saved = own_parts(own)
        keep, *sent = y_first(own_sums, own_saved, shift(other, "core", 1))
        pair = [(i, i ^ 1) for i in range(ny)]
        mirror = [(i, ny - 1 - i) for i in range(ny)]
        received = [lax.ppermute(sent[0], "y", pair), lax.ppermute(sent[1], "y", mirror)]
        total, *sent = y_second(keep, sent, received)
        received = [lax.ppermute(sent[0], "y", mirror), lax.ppermute(sent[1], "y", pair)]
        mids, saved_rows = mid_grads(total, sent, received)
        mids_other = shift(mids, "core", 1)
    with jax.named_scope("terms_over_first"):
        terms = products(
            jobs, block_fill, slot_of, tokens, mids, mids_other, saved_rows, cotangent, parts
        )
        terms = lax.all_to_all(terms, FIRST, split_axis=0, concat_axis=0, tiled=True)
    with jax.named_scope("keys_core"):
        keys_own, keys_other = keys_partials(
            place, jobs, tokens, frozen_weight, saved_rows, up_stack
        )
        keys_parts = keys_chip_sums(keys_own, shift(keys_other, "core", 1))
        terms, keys_parts = lax.optimization_barrier((terms, keys_parts))
    with jax.named_scope("keys_y"):
        keys = keys_parts[0]
        for d in range(1, ny):
            keys = keys + shift(keys_parts[d], "y", d)
        keys = keys.astype(BF16)
    with jax.named_scope("sums_over_adapter"):
        tail = nblocks * (part + split)
        slots = terms[:, tail : tail + nblocks, 0].astype(jnp.int32)
        sums = slot_sums(slots, terms, slot_count)
        owned = lax.all_to_all(sums, ADAPTER, split_axis=0, concat_axis=0, tiled=True)
    grad_down, grad_up = finish(owned.reshape((nx, nq, npair) + owned.shape[1:]), part)
    return (keys, grad_down.reshape(1, width, rank), grad_up.reshape(1, rank, features))


def solution(mesh):
    chips = Mesh(mesh.devices.reshape(4, 4, 2, 4, 2), ("x", "zq", "zp", "y", "core"))
    return jax.shard_map(
        per_device,
        mesh=chips,
        in_specs=(
            P(ADAPTER, SEQ),
            P(SEQ, None),
            P(ADAPTER + SEQ, None),
            P(ADAPTER, SEQ),
            P(None, None, SEQ),
            P(ADAPTER, None),
            P(ADAPTER),
            P(),
        ),
        out_specs=(
            P(ADAPTER + SEQ, None),
            P(ADAPTER, SEQ, None),
            P(ADAPTER, None, SEQ),
        ),
        check_vma=False,
    )
```

```python
import jax
import jax.numpy as jnp
from jax import lax
from jax.experimental import pallas as pl
from jax.experimental.pallas import tpu as pltpu
from jax.sharding import Mesh, PartitionSpec as P

BLK = 128
ADAPTER_SCALE = 2.0
SEQ = ("y", "core")
FIRST = ("x", "zp")
ADAPTER = ("x", "zq", "zp")
SLOT_ROWS = 16
LIMIT = pltpu.CompilerParams(vmem_limit_bytes=16 * 1024 * 1024)
WHOLE = pltpu.CompilerParams(vmem_limit_bytes=60 * 1024 * 1024)
VMEM = pl.BlockSpec(memory_space=pltpu.VMEM)
SMEM = pl.BlockSpec(memory_space=pltpu.SMEM)
HBM = pl.BlockSpec(memory_space=pltpu.HBM)
BF16 = jnp.bfloat16
F32 = jnp.float32


def shift(value, axis, distance):
    size = lax.axis_size(axis)
    return lax.ppermute(value, axis, [(i, (i + distance) % size) for i in range(size)])


def contract(left, right, left_dim, right_dim):
    return lax.dot_general(
        left, right, (((left_dim,), (right_dim,)), ((), ())), preferred_element_type=F32
    )


def masked(cot_ref, fill_ref, b):
    block = cot_ref[b * BLK : (b + 1) * BLK, :]
    position = lax.broadcasted_iota(jnp.int32, block.shape, 0)
    return jnp.where(position < fill_ref[b], block, jnp.zeros_like(block))


def mid_partials(jobs, fills, up_stack, cotangent, saved):
    nblocks = jobs.shape[0]
    rank, features = up_stack.shape[1:]
    half = nblocks // 2

    def kernel(
        jobs_ref, fill_ref, up_ref, cot_ref, saved_ref, own_ref, other_ref, picked_ref, cot, sems
    ):
        whole = pltpu.make_async_copy(cot_ref, cot, sems.at[nblocks])
        whole.start()
        copies = [
            pltpu.make_async_copy(up_ref.at[jobs_ref[b]], picked_ref.at[b], sems.at[b])
            for b in range(nblocks)
        ]
        for copy in copies:
            copy.start()
        core = lax.axis_index("core")
        own_ref[half] = saved_ref[...].astype(F32)
        other_ref[half] = saved_ref[...].astype(F32)
        whole.wait()
        for copy in copies:
            copy.wait()
        for i in range(half):
            partials = []
            for b in (2 * i, 2 * i + 1):
                partials.append(contract(masked(cot, fill_ref, b), picked_ref[b], 1, 1))
            own_ref[i] = jnp.where(core == 0, partials[0], partials[1])
            other_ref[i] = jnp.where(core == 0, partials[1], partials[0])

    out = jax.ShapeDtypeStruct((half + 1, BLK, rank), F32)
    return pl.pallas_call(
        kernel,
        out_shape=[out, out, jax.ShapeDtypeStruct((nblocks, rank, features), BF16)],
        in_specs=[SMEM, SMEM, HBM, HBM, VMEM],
        out_specs=[VMEM] * 3,
        scratch_shapes=[
            pltpu.VMEM(cotangent.shape, BF16),
            pltpu.SemaphoreType.DMA((nblocks + 1,)),
        ],
        compiler_params=WHOLE,
        name="mid_partials",
    )(jobs, fills, up_stack, cotangent, saved)


def halves_of(total):
    high = total.astype(BF16)
    return high, (total - high.astype(F32)).astype(BF16)


def own_parts(own):
    half, _, rank = own.shape
    half -= 1

    def kernel(own_ref, sums_ref, saved_ref):
        sums_ref[...] = own_ref[:half]
        saved_ref[...] = own_ref[half].astype(BF16)

    return pl.pallas_call(
        kernel,
        out_shape=[
            jax.ShapeDtypeStruct((half, BLK, rank), F32),
            jax.ShapeDtypeStruct((BLK, rank), BF16),
        ],
        in_specs=[VMEM],
        out_specs=[VMEM] * 2,
        compiler_params=LIMIT,
        name="own_parts",
    )(own)


def y_first(own, saved, received):
    half, _, rank = own.shape
    each = half // 2

    def kernel(own_ref, saved_ref, received_ref, keep_ref, *outs):
        first = lax.axis_index("core") == 0
        mine, theirs = saved_ref[...], received_ref[half].astype(BF16)
        total = own_ref[...] + received_ref[:half]
        keep_ref[...] = total
        for i, out in enumerate(outs):
            out[:each], out[each : 2 * each] = halves_of(total[i * each : (i + 1) * each])
            out[2 * each] = jnp.where(first, *((mine, theirs) if i == 0 else (theirs, mine)))

    return pl.pallas_call(
        kernel,
        out_shape=[jax.ShapeDtypeStruct((half, BLK, rank), F32)]
        + [jax.ShapeDtypeStruct((2 * each + 1, BLK, rank), BF16)] * 2,
        in_specs=[VMEM] * 3,
        out_specs=[VMEM] * 3,
        compiler_params=LIMIT,
        name="y_first",
    )(own, saved, received)


def y_second(keep, sent, received):
    half, _, rank = keep.shape
    each = half // 2

    def kernel(keep_ref, *refs):
        sent_refs, got_refs, total_ref, outs = refs[:2], refs[2:4], refs[4], refs[5:]
        for i in range(2):
            got = got_refs[i]
            blocks = slice(i * each, (i + 1) * each)
            total = keep_ref[blocks] + got[:each].astype(F32) + got[each : 2 * each].astype(F32)
            total_ref[blocks] = total
            outs[i][:each], outs[i][each : 2 * each] = halves_of(total)
            outs[i][2 * each] = sent_refs[i][2 * each]
            outs[i][2 * each + 1] = got[2 * each]

    return pl.pallas_call(
        kernel,
        out_shape=[jax.ShapeDtypeStruct(keep.shape, F32)]
        + [jax.ShapeDtypeStruct((2 * each + 2, BLK, rank), BF16)] * 2,
        in_specs=[VMEM] * 5,
        out_specs=[VMEM] * 3,
        compiler_params=LIMIT,
        name="y_second",
    )(keep, *sent, *received)


def mid_grads(total, sent, received):
    half, _, rank = total.shape
    each = half // 2

    def kernel(total_ref, *refs):
        sent_refs, got_refs, mids_ref, rows_ref = refs[:2], refs[2:4], refs[4], refs[5]
        y = lax.axis_index("y")
        pair, mirror = lax.bitwise_xor(y, 1), half - 1 - y
        for i, (near, far) in enumerate(((pair, mirror), (mirror, pair))):
            got = got_refs[i]
            blocks = slice(i * each, (i + 1) * each)
            mids_ref[blocks] = (
                total_ref[blocks] + got[:each].astype(F32) + got[each : 2 * each].astype(F32)
            ).astype(BF16)
            beyond = lax.bitwise_xor(far, 1) if i == 0 else half - 1 - far
            rows_ref[2 * y + i] = sent_refs[i][2 * each]
            rows_ref[2 * near + i] = sent_refs[i][2 * each + 1]
            rows_ref[2 * far + i] = got[2 * each]
            rows_ref[2 * beyond + i] = got[2 * each + 1]

    return pl.pallas_call(
        kernel,
        out_shape=[
            jax.ShapeDtypeStruct((half, BLK, rank), BF16),
            jax.ShapeDtypeStruct((2 * half, BLK, rank), BF16),
        ],
        in_specs=[VMEM] * 5,
        out_specs=[VMEM] * 2,
        compiler_params=LIMIT,
        name="mid_grads",
    )(total, *sent, *received)


def products(jobs, fills, slot_of, tokens, mids, mids_other, saved_rows, cotangent, parts):
    width = tokens.shape[1]
    nblocks, _, rank = saved_rows.shape
    part, split = width // parts, rank // parts
    height = part + split

    def kernel(
        jobs_ref, fill_ref, slot_ref, tokens_ref, mids_ref, other_ref, saved_ref, cot_ref, out_ref
    ):
        core = lax.axis_index("core")
        row = lax.broadcasted_iota(jnp.int32, (SLOT_ROWS, rank), 0)
        slots = jnp.zeros((SLOT_ROWS, rank), jnp.int32)
        for b in range(nblocks):
            slots = jnp.where(row == b, slot_ref[jobs_ref[b]], slots)
        slots = slots.astype(F32).astype(BF16)
        for i in range(parts):
            out_ref[i, nblocks * height :, :] = slots
        for b in range(nblocks):
            mine, other = mids_ref[b // 2], other_ref[b // 2]
            mid = jnp.where(core == b % 2, mine, other)
            up = contract(saved_ref[b], masked(cot_ref, fill_ref, b), 0, 0).astype(BF16)
            first = b * height
            for i in range(parts):
                block = tokens_ref[b * BLK : (b + 1) * BLK, i * part : (i + 1) * part]
                out_ref[i, first : first + part, :] = contract(block, mid, 0, 0).astype(BF16)
                out_ref[i, first + part : first + height, :] = up[i * split : (i + 1) * split]

    return pl.pallas_call(
        kernel,
        out_shape=jax.ShapeDtypeStruct((parts, nblocks * height + SLOT_ROWS, rank), BF16),
        in_specs=[SMEM] * 3 + [VMEM] * 5,
        out_specs=VMEM,
        compiler_params=LIMIT,
        name="products",
    )(jobs, fills, slot_of, tokens, mids, mids_other, saved_rows, cotangent)


def slot_sums(slots, terms, slot_count):
    groups, nblocks = slots.shape
    rank = terms.shape[2]
    height = (terms.shape[1] - SLOT_ROWS) // nblocks

    def kernel(slots_ref, terms_ref, out_ref, acc):
        acc[...] = jnp.zeros_like(acc)
        for g in range(groups):
            for b in range(nblocks):
                acc[slots_ref[g, b]] += terms_ref[g, b * height : (b + 1) * height, :].astype(F32)
        out_ref[...] = acc[...].astype(BF16)

    return pl.pallas_call(
        kernel,
        out_shape=jax.ShapeDtypeStruct((slot_count, height, rank), BF16),
        in_specs=[SMEM, VMEM],
        out_specs=VMEM,
        scratch_shapes=[pltpu.VMEM((slot_count, height, rank), F32)],
        compiler_params=LIMIT,
        name="slot_sums",
    )(slots, terms)


def finish(owned, part):
    nx, nq, npair, height, rank = owned.shape
    parts, split = nx * npair, height - part

    def kernel(owned_ref, down_ref, up_ref):
        for x in range(nx):
            for p in range(npair):
                total = owned_ref[x, 0, p].astype(F32)
                for q in range(1, nq):
                    total += owned_ref[x, q, p].astype(F32)
                total = ADAPTER_SCALE * total
                down_ref[x * npair + p] = total[:part]
                up_ref[x * npair + p] = total[part:]

    return pl.pallas_call(
        kernel,
        out_shape=[
            jax.ShapeDtypeStruct((parts, part, rank), F32),
            jax.ShapeDtypeStruct((parts, split, rank), F32),
        ],
        in_specs=[VMEM],
        out_specs=[VMEM, VMEM],
        compiler_params=LIMIT,
        name="finish",
    )(owned)


def keys_partials(place, tokens, frozen_weight, saved_rows, picked):
    rows, width = tokens.shape
    nblocks, rank, features = picked.shape
    half = nblocks // 2
    total = frozen_weight.shape[1]

    def block_of(i, j, place_ref):
        return 2 * j + lax.rem(place_ref[1] + i, 2)

    def kernel(place_ref, tokens_ref, weight_ref, saved_ref, picked_ref, own_ref, other_ref):
        columns = pl.ds(pl.multiple_of((2 * place_ref[0] + place_ref[1]) * features, features), features)
        for i, out_ref in enumerate((own_ref, other_ref)):

            @pl.when(pl.program_id(0) == i)
            def _():
                out_ref[0] = jnp.dot(tokens_ref[...], weight_ref[...], preferred_element_type=F32)
                out_ref[0, :, columns] += ADAPTER_SCALE * jnp.dot(
                    saved_ref[0], picked_ref[0], preferred_element_type=F32
                )

    shape = jax.ShapeDtypeStruct((half, BLK, total), F32)
    return pl.pallas_call(
        kernel,
        grid_spec=pltpu.PrefetchScalarGridSpec(
            num_scalar_prefetch=1,
            grid=(2, half),
            in_specs=[
                pl.BlockSpec((BLK, width), lambda i, j, place: (block_of(i, j, place), 0)),
                pl.BlockSpec((width, total), lambda i, j, place: (0, 0)),
                pl.BlockSpec((1, BLK, rank), lambda i, j, place: (block_of(i, j, place), 0, 0)),
                pl.BlockSpec((1, rank, features), lambda i, j, place: (block_of(i, j, place), 0, 0)),
            ],
            out_specs=[
                pl.BlockSpec((1, BLK, total), lambda i, j, place: (jnp.where(i == 0, j, half - 1), 0, 0)),
                pl.BlockSpec((1, BLK, total), lambda i, j, place: (jnp.where(i == 0, 0, j), 0, 0)),
            ],
        ),
        out_shape=[shape, shape],
        compiler_params=LIMIT,
        name="keys_partials",
    )(place, tokens, frozen_weight, saved_rows, picked)


def keys_chip_sums(own, received):
    ny, block, total = own.shape

    def kernel(own_ref, received_ref, *outs):
        for d in range(ny):
            to = lax.rem(lax.axis_index("y") + d, ny)
            outs[d][...] = own_ref[to] + received_ref[to]

    return pl.pallas_call(
        kernel,
        out_shape=[jax.ShapeDtypeStruct((block, total), F32)] * ny,
        in_specs=[VMEM, VMEM],
        out_specs=[VMEM] * ny,
        compiler_params=LIMIT,
        name="keys_chip_sums",
    )(own, received)


def per_device(
    tokens, frozen_weight, saved_mid, cotangent, up_stack, block_job, block_fill, slot_of
):
    width = tokens.shape[1]
    features = cotangent.shape[1]
    rank = saved_mid.shape[1]
    nblocks = block_job.shape[0]
    slot_count = slot_of.shape[0]
    nx, nq, npair, ny = (lax.axis_size(name) for name in ADAPTER + ("y",))
    parts = nx * npair
    part, split = width // parts, rank // parts
    jobs = block_job.reshape(nblocks)
    place = jnp.stack([lax.axis_index(name) for name in SEQ]).astype(jnp.int32)

    with jax.named_scope("mid_sums"):
        own, other, picked = mid_partials(jobs, block_fill, up_stack, cotangent, saved_mid)
        own_sums, own_saved = own_parts(own)
        keep, *sent = y_first(own_sums, own_saved, shift(other, "core", 1))
        pair = [(i, i ^ 1) for i in range(ny)]
        mirror = [(i, ny - 1 - i) for i in range(ny)]
        received = [lax.ppermute(sent[0], "y", pair), lax.ppermute(sent[1], "y", mirror)]
        total, *sent = y_second(keep, sent, received)
        received = [lax.ppermute(sent[0], "y", mirror), lax.ppermute(sent[1], "y", pair)]
        mids, saved_rows = mid_grads(total, sent, received)
        mids_other = shift(mids, "core", 1)
    with jax.named_scope("terms_over_first"):
        terms = products(
            jobs, block_fill, slot_of, tokens, mids, mids_other, saved_rows, cotangent, parts
        )
        terms = lax.all_to_all(terms, FIRST, split_axis=0, concat_axis=0, tiled=True)
    with jax.named_scope("keys_core"):
        keys_own, keys_other = keys_partials(place, tokens, frozen_weight, saved_rows, picked)
        keys_parts = keys_chip_sums(keys_own, shift(keys_other, "core", 1))
        terms, keys_parts = lax.optimization_barrier((terms, keys_parts))
    with jax.named_scope("keys_y"):
        keys = keys_parts[0]
        for d in range(1, ny):
            keys = keys + shift(keys_parts[d], "y", d)
        keys = keys.astype(BF16)
    with jax.named_scope("sums_over_adapter"):
        tail = nblocks * (part + split)
        slots = terms[:, tail : tail + nblocks, 0].astype(jnp.int32)
        sums = slot_sums(slots, terms, slot_count)
        owned = lax.all_to_all(sums, ADAPTER, split_axis=0, concat_axis=0, tiled=True)
    grad_down, grad_up = finish(owned.reshape((nx, nq, npair) + owned.shape[1:]), part)
    return (keys, grad_down.reshape(1, width, rank), grad_up.reshape(1, rank, features))


def solution(mesh):
    chips = Mesh(mesh.devices.reshape(4, 4, 2, 4, 2), ("x", "zq", "zp", "y", "core"))
    return jax.shard_map(
        per_device,
        mesh=chips,
        in_specs=(
            P(ADAPTER, SEQ),
            P(SEQ, None),
            P(ADAPTER + SEQ, None),
            P(ADAPTER, SEQ),
            P(None, None, SEQ),
            P(ADAPTER, None),
            P(ADAPTER),
            P(),
        ),
        out_specs=(
            P(ADAPTER + SEQ, None),
            P(ADAPTER, SEQ, None),
            P(ADAPTER, None, SEQ),
        ),
        check_vma=False,
    )
```

```python
import jax
import jax.numpy as jnp
from jax import lax
from jax.experimental import pallas as pl
from jax.experimental.pallas import tpu as pltpu
from jax.sharding import Mesh, PartitionSpec as P

BLK = 128
ADAPTER_SCALE = 2.0
SEQ = ("y", "core")
FIRST = ("x", "zp")
ADAPTER = ("x", "zq", "zp")
SLOT_ROWS = 16
LIMIT = pltpu.CompilerParams(vmem_limit_bytes=16 * 1024 * 1024)
WHOLE = pltpu.CompilerParams(vmem_limit_bytes=60 * 1024 * 1024)
VMEM = pl.BlockSpec(memory_space=pltpu.VMEM)
SMEM = pl.BlockSpec(memory_space=pltpu.SMEM)
HBM = pl.BlockSpec(memory_space=pltpu.HBM)
BF16 = jnp.bfloat16
F32 = jnp.float32


def shift(value, axis, distance):
    size = lax.axis_size(axis)
    return lax.ppermute(value, axis, [(i, (i + distance) % size) for i in range(size)])


def contract(left, right, left_dim, right_dim):
    return lax.dot_general(
        left, right, (((left_dim,), (right_dim,)), ((), ())), preferred_element_type=F32
    )


def masked(cot_ref, fill_ref, b):
    block = cot_ref[b * BLK : (b + 1) * BLK, :]
    position = lax.broadcasted_iota(jnp.int32, block.shape, 0)
    return jnp.where(position < fill_ref[b], block, jnp.zeros_like(block))


def mid_partials(jobs, fills, up_stack, cotangent, saved):
    nblocks = jobs.shape[0]
    rank, features = up_stack.shape[1:]
    half = nblocks // 2

    def kernel(
        jobs_ref, fill_ref, up_ref, cot_ref, saved_ref, own_ref, other_ref, picked_ref, cot, sems
    ):
        whole = pltpu.make_async_copy(cot_ref, cot, sems.at[nblocks])
        whole.start()
        copies = [
            pltpu.make_async_copy(up_ref.at[jobs_ref[b]], picked_ref.at[b], sems.at[b])
            for b in range(nblocks)
        ]
        for copy in copies:
            copy.start()
        core = lax.axis_index("core")
        own_ref[half] = saved_ref[...].astype(F32)
        other_ref[half] = saved_ref[...].astype(F32)
        whole.wait()
        for copy in copies:
            copy.wait()
        for i in range(half):
            partials = []
            for b in (2 * i, 2 * i + 1):
                partials.append(contract(masked(cot, fill_ref, b), picked_ref[b], 1, 1))
            own_ref[i] = jnp.where(core == 0, partials[0], partials[1])
            other_ref[i] = jnp.where(core == 0, partials[1], partials[0])

    out = jax.ShapeDtypeStruct((half + 1, BLK, rank), F32)
    return pl.pallas_call(
        kernel,
        out_shape=[out, out, jax.ShapeDtypeStruct((nblocks, rank, features), BF16)],
        in_specs=[SMEM, SMEM, HBM, HBM, VMEM],
        out_specs=[VMEM] * 3,
        scratch_shapes=[
            pltpu.VMEM(cotangent.shape, BF16),
            pltpu.SemaphoreType.DMA((nblocks + 1,)),
        ],
        compiler_params=WHOLE,
        name="mid_partials",
    )(jobs, fills, up_stack, cotangent, saved)


def halves_of(total):
    high = total.astype(BF16)
    return high, (total - high.astype(F32)).astype(BF16)


def own_parts(own):
    half, _, rank = own.shape
    half -= 1

    def kernel(own_ref, sums_ref, saved_ref):
        sums_ref[...] = own_ref[:half]
        saved_ref[...] = own_ref[half].astype(BF16)

    return pl.pallas_call(
        kernel,
        out_shape=[
            jax.ShapeDtypeStruct((half, BLK, rank), F32),
            jax.ShapeDtypeStruct((BLK, rank), BF16),
        ],
        in_specs=[VMEM],
        out_specs=[VMEM] * 2,
        compiler_params=LIMIT,
        name="own_parts",
    )(own)


def y_first(own, saved, received):
    half, _, rank = own.shape
    each = half // 2

    def kernel(own_ref, saved_ref, received_ref, keep_ref, *outs):
        first = lax.axis_index("core") == 0
        mine, theirs = saved_ref[...], received_ref[half].astype(BF16)
        total = own_ref[...] + received_ref[:half]
        keep_ref[...] = total
        for i, out in enumerate(outs):
            out[:each], out[each : 2 * each] = halves_of(total[i * each : (i + 1) * each])
            out[2 * each] = jnp.where(first, *((mine, theirs) if i == 0 else (theirs, mine)))

    return pl.pallas_call(
        kernel,
        out_shape=[jax.ShapeDtypeStruct((half, BLK, rank), F32)]
        + [jax.ShapeDtypeStruct((2 * each + 1, BLK, rank), BF16)] * 2,
        in_specs=[VMEM] * 3,
        out_specs=[VMEM] * 3,
        compiler_params=LIMIT,
        name="y_first",
    )(own, saved, received)


def y_second(keep, sent, received):
    half, _, rank = keep.shape
    each = half // 2

    def kernel(keep_ref, *refs):
        sent_refs, got_refs, total_ref, outs = refs[:2], refs[2:4], refs[4], refs[5:]
        for i in range(2):
            got = got_refs[i]
            blocks = slice(i * each, (i + 1) * each)
            total = keep_ref[blocks] + got[:each].astype(F32) + got[each : 2 * each].astype(F32)
            total_ref[blocks] = total
            outs[i][:each], outs[i][each : 2 * each] = halves_of(total)
            outs[i][2 * each] = sent_refs[i][2 * each]
            outs[i][2 * each + 1] = got[2 * each]

    return pl.pallas_call(
        kernel,
        out_shape=[jax.ShapeDtypeStruct(keep.shape, F32)]
        + [jax.ShapeDtypeStruct((2 * each + 2, BLK, rank), BF16)] * 2,
        in_specs=[VMEM] * 5,
        out_specs=[VMEM] * 3,
        compiler_params=LIMIT,
        name="y_second",
    )(keep, *sent, *received)


def mid_grads(total, sent, received):
    half, _, rank = total.shape
    each = half // 2

    def kernel(total_ref, *refs):
        sent_refs, got_refs, mids_ref, rows_ref = refs[:2], refs[2:4], refs[4], refs[5]
        y = lax.axis_index("y")
        pair, mirror = lax.bitwise_xor(y, 1), half - 1 - y
        for i, (near, far) in enumerate(((pair, mirror), (mirror, pair))):
            got = got_refs[i]
            blocks = slice(i * each, (i + 1) * each)
            mids_ref[blocks] = (
                total_ref[blocks] + got[:each].astype(F32) + got[each : 2 * each].astype(F32)
            ).astype(BF16)
            beyond = lax.bitwise_xor(far, 1) if i == 0 else half - 1 - far
            rows_ref[2 * y + i] = sent_refs[i][2 * each]
            rows_ref[2 * near + i] = sent_refs[i][2 * each + 1]
            rows_ref[2 * far + i] = got[2 * each]
            rows_ref[2 * beyond + i] = got[2 * each + 1]

    return pl.pallas_call(
        kernel,
        out_shape=[
            jax.ShapeDtypeStruct((half, BLK, rank), BF16),
            jax.ShapeDtypeStruct((2 * half, BLK, rank), BF16),
        ],
        in_specs=[VMEM] * 5,
        out_specs=[VMEM] * 2,
        compiler_params=LIMIT,
        name="mid_grads",
    )(total, *sent, *received)


def up_products(jobs, fills, slot_of, saved_rows, cotangent):
    nblocks, _, rank = saved_rows.shape

    def kernel(jobs_ref, fill_ref, slot_ref, saved_ref, cot_ref, up_ref, slots_ref):
        row = lax.broadcasted_iota(jnp.int32, (SLOT_ROWS, rank), 0)
        slots = jnp.zeros((SLOT_ROWS, rank), jnp.int32)
        for b in range(nblocks):
            slots = jnp.where(row == b, slot_ref[jobs_ref[b]], slots)
            up_ref[b] = contract(saved_ref[b], masked(cot_ref, fill_ref, b), 0, 0).astype(BF16)
        slots_ref[...] = slots.astype(F32).astype(BF16)

    return pl.pallas_call(
        kernel,
        out_shape=[
            jax.ShapeDtypeStruct((nblocks, rank, cotangent.shape[1]), BF16),
            jax.ShapeDtypeStruct((SLOT_ROWS, rank), BF16),
        ],
        in_specs=[SMEM] * 3 + [VMEM] * 2,
        out_specs=[VMEM] * 2,
        compiler_params=LIMIT,
        name="up_products",
    )(jobs, fills, slot_of, saved_rows, cotangent)


def products(tokens, mids, mids_other, ups, slot_rows, parts):
    width = tokens.shape[1]
    nblocks, rank, _ = ups.shape
    part, split = width // parts, rank // parts
    height = part + split

    def kernel(tokens_ref, mids_ref, other_ref, up_ref, slots_ref, out_ref):
        core = lax.axis_index("core")
        for i in range(parts):
            out_ref[i, nblocks * height :, :] = slots_ref[...]
        for b in range(nblocks):
            mid = jnp.where(core == b % 2, mids_ref[b // 2], other_ref[b // 2])
            first = b * height
            for i in range(parts):
                block = tokens_ref[b * BLK : (b + 1) * BLK, i * part : (i + 1) * part]
                out_ref[i, first : first + part, :] = contract(block, mid, 0, 0).astype(BF16)
                out_ref[i, first + part : first + height, :] = up_ref[b, i * split : (i + 1) * split]

    return pl.pallas_call(
        kernel,
        out_shape=jax.ShapeDtypeStruct((parts, nblocks * height + SLOT_ROWS, rank), BF16),
        in_specs=[VMEM] * 5,
        out_specs=VMEM,
        compiler_params=LIMIT,
        name="products",
    )(tokens, mids, mids_other, ups, slot_rows)


def slot_sums(slots, terms, slot_count):
    groups, nblocks = slots.shape
    rank = terms.shape[2]
    height = (terms.shape[1] - SLOT_ROWS) // nblocks

    def kernel(slots_ref, terms_ref, out_ref, acc):
        acc[...] = jnp.zeros_like(acc)
        for g in range(groups):
            for b in range(nblocks):
                acc[slots_ref[g, b]] += terms_ref[g, b * height : (b + 1) * height, :].astype(F32)
        out_ref[...] = acc[...].astype(BF16)

    return pl.pallas_call(
        kernel,
        out_shape=jax.ShapeDtypeStruct((slot_count, height, rank), BF16),
        in_specs=[SMEM, VMEM],
        out_specs=VMEM,
        scratch_shapes=[pltpu.VMEM((slot_count, height, rank), F32)],
        compiler_params=LIMIT,
        name="slot_sums",
    )(slots, terms)


def finish(owned, part):
    nx, nq, npair, height, rank = owned.shape
    parts, split = nx * npair, height - part

    def kernel(owned_ref, down_ref, up_ref):
        for x in range(nx):
            for p in range(npair):
                total = owned_ref[x, 0, p].astype(F32)
                for q in range(1, nq):
                    total += owned_ref[x, q, p].astype(F32)
                total = ADAPTER_SCALE * total
                down_ref[x * npair + p] = total[:part]
                up_ref[x * npair + p] = total[part:]

    return pl.pallas_call(
        kernel,
        out_shape=[
            jax.ShapeDtypeStruct((parts, part, rank), F32),
            jax.ShapeDtypeStruct((parts, split, rank), F32),
        ],
        in_specs=[VMEM],
        out_specs=[VMEM, VMEM],
        compiler_params=LIMIT,
        name="finish",
    )(owned)


def keys_partials(place, tokens, frozen_weight, saved_rows, picked):
    rows, width = tokens.shape
    nblocks, rank, features = picked.shape
    half = nblocks // 2
    total = frozen_weight.shape[1]

    def block_of(i, j, place_ref):
        return 2 * j + lax.rem(place_ref[1] + i, 2)

    def kernel(place_ref, tokens_ref, weight_ref, saved_ref, picked_ref, own_ref, other_ref):
        columns = pl.ds(pl.multiple_of((2 * place_ref[0] + place_ref[1]) * features, features), features)
        for i, out_ref in enumerate((own_ref, other_ref)):

            @pl.when(pl.program_id(0) == i)
            def _():
                out_ref[0] = jnp.dot(tokens_ref[...], weight_ref[...], preferred_element_type=F32)
                out_ref[0, :, columns] += ADAPTER_SCALE * jnp.dot(
                    saved_ref[0], picked_ref[0], preferred_element_type=F32
                )

    shape = jax.ShapeDtypeStruct((half, BLK, total), F32)
    return pl.pallas_call(
        kernel,
        grid_spec=pltpu.PrefetchScalarGridSpec(
            num_scalar_prefetch=1,
            grid=(2, half),
            in_specs=[
                pl.BlockSpec((BLK, width), lambda i, j, place: (block_of(i, j, place), 0)),
                pl.BlockSpec((width, total), lambda i, j, place: (0, 0)),
                pl.BlockSpec((1, BLK, rank), lambda i, j, place: (block_of(i, j, place), 0, 0)),
                pl.BlockSpec((1, rank, features), lambda i, j, place: (block_of(i, j, place), 0, 0)),
            ],
            out_specs=[
                pl.BlockSpec((1, BLK, total), lambda i, j, place: (jnp.where(i == 0, j, half - 1), 0, 0)),
                pl.BlockSpec((1, BLK, total), lambda i, j, place: (jnp.where(i == 0, 0, j), 0, 0)),
            ],
        ),
        out_shape=[shape, shape],
        compiler_params=LIMIT,
        name="keys_partials",
    )(place, tokens, frozen_weight, saved_rows, picked)


def keys_chip_sums(own, received):
    ny, block, total = own.shape

    def kernel(own_ref, received_ref, *outs):
        for d in range(ny):
            to = lax.rem(lax.axis_index("y") + d, ny)
            outs[d][...] = own_ref[to] + received_ref[to]

    return pl.pallas_call(
        kernel,
        out_shape=[jax.ShapeDtypeStruct((block, total), F32)] * ny,
        in_specs=[VMEM, VMEM],
        out_specs=[VMEM] * ny,
        compiler_params=LIMIT,
        name="keys_chip_sums",
    )(own, received)


def per_device(
    tokens, frozen_weight, saved_mid, cotangent, up_stack, block_job, block_fill, slot_of
):
    width = tokens.shape[1]
    features = cotangent.shape[1]
    rank = saved_mid.shape[1]
    nblocks = block_job.shape[0]
    slot_count = slot_of.shape[0]
    nx, nq, npair, ny = (lax.axis_size(name) for name in ADAPTER + ("y",))
    parts = nx * npair
    part, split = width // parts, rank // parts
    jobs = block_job.reshape(nblocks)
    place = jnp.stack([lax.axis_index(name) for name in SEQ]).astype(jnp.int32)

    with jax.named_scope("mid_sums"):
        own, other, picked = mid_partials(jobs, block_fill, up_stack, cotangent, saved_mid)
        own_sums, own_saved = own_parts(own)
        keep, *sent = y_first(own_sums, own_saved, shift(other, "core", 1))
        pair = [(i, i ^ 1) for i in range(ny)]
        mirror = [(i, ny - 1 - i) for i in range(ny)]
        received = [lax.ppermute(sent[0], "y", pair), lax.ppermute(sent[1], "y", mirror)]
        total, *sent = y_second(keep, sent, received)
        received = [lax.ppermute(sent[0], "y", mirror), lax.ppermute(sent[1], "y", pair)]
        mids, saved_rows = mid_grads(total, sent, received)
        mids_other = shift(mids, "core", 1)
    with jax.named_scope("terms_over_first"):
        ups, slot_rows = up_products(jobs, block_fill, slot_of, saved_rows, cotangent)
        terms = products(tokens, mids, mids_other, ups, slot_rows, parts)
        terms = lax.all_to_all(terms, FIRST, split_axis=0, concat_axis=0, tiled=True)
    with jax.named_scope("keys_core"):
        keys_own, keys_other = keys_partials(place, tokens, frozen_weight, saved_rows, picked)
        keys_parts = keys_chip_sums(keys_own, shift(keys_other, "core", 1))
        terms, keys_parts = lax.optimization_barrier((terms, keys_parts))
    with jax.named_scope("keys_y"):
        keys = keys_parts[0]
        for d in range(1, ny):
            keys = keys + shift(keys_parts[d], "y", d)
        keys = keys.astype(BF16)
    with jax.named_scope("sums_over_adapter"):
        tail = nblocks * (part + split)
        slots = terms[:, tail : tail + nblocks, 0].astype(jnp.int32)
        sums = slot_sums(slots, terms, slot_count)
        owned = lax.all_to_all(sums, ADAPTER, split_axis=0, concat_axis=0, tiled=True)
    grad_down, grad_up = finish(owned.reshape((nx, nq, npair) + owned.shape[1:]), part)
    return (keys, grad_down.reshape(1, width, rank), grad_up.reshape(1, rank, features))


def solution(mesh):
    chips = Mesh(mesh.devices.reshape(4, 4, 2, 4, 2), ("x", "zq", "zp", "y", "core"))
    return jax.shard_map(
        per_device,
        mesh=chips,
        in_specs=(
            P(ADAPTER, SEQ),
            P(SEQ, None),
            P(ADAPTER + SEQ, None),
            P(ADAPTER, SEQ),
            P(None, None, SEQ),
            P(ADAPTER, None),
            P(ADAPTER),
            P(),
        ),
        out_specs=(
            P(ADAPTER + SEQ, None),
            P(ADAPTER, SEQ, None),
            P(ADAPTER, None, SEQ),
        ),
        check_vma=False,
    )
```

```python
import jax
import jax.numpy as jnp
from jax import lax
from jax.experimental import pallas as pl
from jax.experimental.pallas import tpu as pltpu
from jax.sharding import Mesh, PartitionSpec as P

BLK = 128
ADAPTER_SCALE = 2.0
SEQ = ("y", "core")
FIRST = ("x", "zp")
ADAPTER = ("x", "zq", "zp")
SLOT_ROWS = 16
LIMIT = pltpu.CompilerParams(vmem_limit_bytes=16 * 1024 * 1024)
WHOLE = pltpu.CompilerParams(vmem_limit_bytes=60 * 1024 * 1024)
VMEM = pl.BlockSpec(memory_space=pltpu.VMEM)
SMEM = pl.BlockSpec(memory_space=pltpu.SMEM)
HBM = pl.BlockSpec(memory_space=pltpu.HBM)
BF16 = jnp.bfloat16
F32 = jnp.float32


def shift(value, axis, distance):
    size = lax.axis_size(axis)
    return lax.ppermute(value, axis, [(i, (i + distance) % size) for i in range(size)])


def contract(left, right, left_dim, right_dim):
    return lax.dot_general(
        left, right, (((left_dim,), (right_dim,)), ((), ())), preferred_element_type=F32
    )


def masked(cot_ref, fill_ref, b):
    block = cot_ref[b * BLK : (b + 1) * BLK, :]
    position = lax.broadcasted_iota(jnp.int32, block.shape, 0)
    return jnp.where(position < fill_ref[b], block, jnp.zeros_like(block))


def mid_partials(jobs, fills, up_stack, cotangent, saved):
    nblocks = jobs.shape[0]
    rank, features = up_stack.shape[1:]
    half = nblocks // 2

    def kernel(
        jobs_ref, fill_ref, up_ref, cot_ref, saved_ref, own_ref, other_ref, picked_ref, cot, sems
    ):
        whole = pltpu.make_async_copy(cot_ref, cot, sems.at[nblocks])
        whole.start()
        copies = [
            pltpu.make_async_copy(up_ref.at[jobs_ref[b]], picked_ref.at[b], sems.at[b])
            for b in range(nblocks)
        ]
        for copy in copies:
            copy.start()
        core = lax.axis_index("core")
        own_ref[half] = saved_ref[...].astype(F32)
        other_ref[half] = saved_ref[...].astype(F32)
        whole.wait()
        for copy in copies:
            copy.wait()
        for i in range(half):
            partials = []
            for b in (2 * i, 2 * i + 1):
                partials.append(contract(masked(cot, fill_ref, b), picked_ref[b], 1, 1))
            own_ref[i] = jnp.where(core == 0, partials[0], partials[1])
            other_ref[i] = jnp.where(core == 0, partials[1], partials[0])

    out = jax.ShapeDtypeStruct((half + 1, BLK, rank), F32)
    return pl.pallas_call(
        kernel,
        out_shape=[out, out, jax.ShapeDtypeStruct((nblocks, rank, features), BF16)],
        in_specs=[SMEM, SMEM, HBM, HBM, VMEM],
        out_specs=[VMEM] * 3,
        scratch_shapes=[
            pltpu.VMEM(cotangent.shape, BF16),
            pltpu.SemaphoreType.DMA((nblocks + 1,)),
        ],
        compiler_params=WHOLE,
        name="mid_partials",
    )(jobs, fills, up_stack, cotangent, saved)


def halves_of(total):
    high = total.astype(BF16)
    return high, (total - high.astype(F32)).astype(BF16)


def own_parts(own):
    half, _, rank = own.shape
    half -= 1

    def kernel(own_ref, sums_ref, saved_ref):
        sums_ref[...] = own_ref[:half]
        saved_ref[...] = own_ref[half].astype(BF16)

    return pl.pallas_call(
        kernel,
        out_shape=[
            jax.ShapeDtypeStruct((half, BLK, rank), F32),
            jax.ShapeDtypeStruct((BLK, rank), BF16),
        ],
        in_specs=[VMEM],
        out_specs=[VMEM] * 2,
        compiler_params=LIMIT,
        name="own_parts",
    )(own)


def y_first(own, saved, received):
    half, _, rank = own.shape
    each = half // 2

    def kernel(own_ref, saved_ref, received_ref, keep_ref, *outs):
        first = lax.axis_index("core") == 0
        mine, theirs = saved_ref[...], received_ref[half].astype(BF16)
        total = own_ref[...] + received_ref[:half]
        keep_ref[...] = total
        for i, out in enumerate(outs):
            out[:each], out[each : 2 * each] = halves_of(total[i * each : (i + 1) * each])
            out[2 * each] = jnp.where(first, *((mine, theirs) if i == 0 else (theirs, mine)))

    return pl.pallas_call(
        kernel,
        out_shape=[jax.ShapeDtypeStruct((half, BLK, rank), F32)]
        + [jax.ShapeDtypeStruct((2 * each + 1, BLK, rank), BF16)] * 2,
        in_specs=[VMEM] * 3,
        out_specs=[VMEM] * 3,
        compiler_params=LIMIT,
        name="y_first",
    )(own, saved, received)


def y_second(keep, sent, received):
    half, _, rank = keep.shape
    each = half // 2

    def kernel(keep_ref, *refs):
        sent_refs, got_refs, total_ref, outs = refs[:2], refs[2:4], refs[4], refs[5:]
        for i in range(2):
            got = got_refs[i]
            blocks = slice(i * each, (i + 1) * each)
            total = keep_ref[blocks] + got[:each].astype(F32) + got[each : 2 * each].astype(F32)
            total_ref[blocks] = total
            outs[i][:each], outs[i][each : 2 * each] = halves_of(total)
            outs[i][2 * each] = sent_refs[i][2 * each]
            outs[i][2 * each + 1] = got[2 * each]

    return pl.pallas_call(
        kernel,
        out_shape=[jax.ShapeDtypeStruct(keep.shape, F32)]
        + [jax.ShapeDtypeStruct((2 * each + 2, BLK, rank), BF16)] * 2,
        in_specs=[VMEM] * 5,
        out_specs=[VMEM] * 3,
        compiler_params=LIMIT,
        name="y_second",
    )(keep, *sent, *received)


def mid_grads(total, sent, received):
    half, _, rank = total.shape
    each = half // 2

    def kernel(total_ref, *refs):
        sent_refs, got_refs, mids_ref, rows_ref = refs[:2], refs[2:4], refs[4], refs[5]
        y = lax.axis_index("y")
        pair, mirror = lax.bitwise_xor(y, 1), half - 1 - y
        for i, (near, far) in enumerate(((pair, mirror), (mirror, pair))):
            got = got_refs[i]
            blocks = slice(i * each, (i + 1) * each)
            mids_ref[blocks] = (
                total_ref[blocks] + got[:each].astype(F32) + got[each : 2 * each].astype(F32)
            ).astype(BF16)
            beyond = lax.bitwise_xor(far, 1) if i == 0 else half - 1 - far
            rows_ref[2 * y + i] = sent_refs[i][2 * each]
            rows_ref[2 * near + i] = sent_refs[i][2 * each + 1]
            rows_ref[2 * far + i] = got[2 * each]
            rows_ref[2 * beyond + i] = got[2 * each + 1]

    return pl.pallas_call(
        kernel,
        out_shape=[
            jax.ShapeDtypeStruct((half, BLK, rank), BF16),
            jax.ShapeDtypeStruct((2 * half, BLK, rank), BF16),
        ],
        in_specs=[VMEM] * 5,
        out_specs=[VMEM] * 2,
        compiler_params=LIMIT,
        name="mid_grads",
    )(total, *sent, *received)


def up_products(jobs, fills, slot_of, saved_rows, cotangent):
    nblocks, _, rank = saved_rows.shape

    def kernel(jobs_ref, fill_ref, slot_ref, saved_ref, cot_ref, up_ref, slots_ref):
        row = lax.broadcasted_iota(jnp.int32, (SLOT_ROWS, rank), 0)
        slots = jnp.zeros((SLOT_ROWS, rank), jnp.int32)
        for b in range(nblocks):
            slots = jnp.where(row == b, slot_ref[jobs_ref[b]], slots)
            up_ref[b] = contract(saved_ref[b], masked(cot_ref, fill_ref, b), 0, 0).astype(BF16)
        slots_ref[...] = slots.astype(F32).astype(BF16)

    return pl.pallas_call(
        kernel,
        out_shape=[
            jax.ShapeDtypeStruct((nblocks, rank, cotangent.shape[1]), BF16),
            jax.ShapeDtypeStruct((SLOT_ROWS, rank), BF16),
        ],
        in_specs=[SMEM] * 3 + [VMEM] * 2,
        out_specs=[VMEM] * 2,
        compiler_params=LIMIT,
        name="up_products",
    )(jobs, fills, slot_of, saved_rows, cotangent)


def products(tokens, mids, mids_other, ups, slot_rows, parts):
    width = tokens.shape[1]
    nblocks, rank, _ = ups.shape
    part, split = width // parts, rank // parts
    height = part + split

    def kernel(tokens_ref, mids_ref, other_ref, up_ref, slots_ref, out_ref):
        core = lax.axis_index("core")
        for i in range(parts):
            out_ref[i, nblocks * height :, :] = slots_ref[...]
        for b in range(nblocks):
            mid = jnp.where(core == b % 2, mids_ref[b // 2], other_ref[b // 2])
            first = b * height
            for i in range(parts):
                block = tokens_ref[b * BLK : (b + 1) * BLK, i * part : (i + 1) * part]
                out_ref[i, first : first + part, :] = contract(block, mid, 0, 0).astype(BF16)
                out_ref[i, first + part : first + height, :] = up_ref[b, i * split : (i + 1) * split]

    return pl.pallas_call(
        kernel,
        out_shape=jax.ShapeDtypeStruct((parts, nblocks * height + SLOT_ROWS, rank), BF16),
        in_specs=[VMEM] * 5,
        out_specs=VMEM,
        compiler_params=LIMIT,
        name="products",
    )(tokens, mids, mids_other, ups, slot_rows)


def slot_sums(slots, terms, slot_count):
    groups, nblocks = slots.shape
    rank = terms.shape[2]
    height = (terms.shape[1] - SLOT_ROWS) // nblocks

    def kernel(slots_ref, terms_ref, out_ref, acc):
        acc[...] = jnp.zeros_like(acc)
        for g in range(groups):
            for b in range(nblocks):
                acc[slots_ref[g, b]] += terms_ref[g, b * height : (b + 1) * height, :].astype(F32)
        out_ref[...] = acc[...].astype(BF16)

    return pl.pallas_call(
        kernel,
        out_shape=jax.ShapeDtypeStruct((slot_count, height, rank), BF16),
        in_specs=[SMEM, VMEM],
        out_specs=VMEM,
        scratch_shapes=[pltpu.VMEM((slot_count, height, rank), F32)],
        compiler_params=LIMIT,
        name="slot_sums",
    )(slots, terms)


def finish(owned, part):
    nx, nq, npair, height, rank = owned.shape
    parts, split = nx * npair, height - part

    def kernel(owned_ref, down_out, up_out, down_ref, up_ref, sems):
        leaving = []
        for x in range(nx):
            for p in range(npair):
                total = owned_ref[x, 0, p].astype(F32)
                for q in range(1, nq):
                    total += owned_ref[x, q, p].astype(F32)
                total = ADAPTER_SCALE * total
                down_ref[x * npair + p] = total[:part]
                up_ref[x * npair + p] = total[part:]
            pieces = slice(x * npair, (x + 1) * npair)
            for i, (source, target) in enumerate(((down_ref, down_out), (up_ref, up_out))):
                copy = pltpu.make_async_copy(
                    source.at[pieces], target.at[pieces], sems.at[2 * x + i]
                )
                copy.start()
                leaving.append(copy)
        for copy in leaving:
            copy.wait()

    return pl.pallas_call(
        kernel,
        out_shape=[
            jax.ShapeDtypeStruct((parts, part, rank), F32),
            jax.ShapeDtypeStruct((parts, split, rank), F32),
        ],
        in_specs=[VMEM],
        out_specs=[HBM, HBM],
        scratch_shapes=[
            pltpu.VMEM((parts, part, rank), F32),
            pltpu.VMEM((parts, split, rank), F32),
            pltpu.SemaphoreType.DMA((2 * nx,)),
        ],
        compiler_params=LIMIT,
        name="finish",
    )(owned)


def keys_partials(place, tokens, frozen_weight, saved_rows, picked):
    rows, width = tokens.shape
    nblocks, rank, features = picked.shape
    half = nblocks // 2
    total = frozen_weight.shape[1]

    def block_of(i, j, place_ref):
        return 2 * j + lax.rem(place_ref[1] + i, 2)

    def kernel(place_ref, tokens_ref, weight_ref, saved_ref, picked_ref, own_ref, other_ref):
        columns = pl.ds(pl.multiple_of((2 * place_ref[0] + place_ref[1]) * features, features), features)
        for i, out_ref in enumerate((own_ref, other_ref)):

            @pl.when(pl.program_id(0) == i)
            def _():
                out_ref[0] = jnp.dot(tokens_ref[...], weight_ref[...], preferred_element_type=F32)
                out_ref[0, :, columns] += ADAPTER_SCALE * jnp.dot(
                    saved_ref[0], picked_ref[0], preferred_element_type=F32
                )

    shape = jax.ShapeDtypeStruct((half, BLK, total), F32)
    return pl.pallas_call(
        kernel,
        grid_spec=pltpu.PrefetchScalarGridSpec(
            num_scalar_prefetch=1,
            grid=(2, half),
            in_specs=[
                pl.BlockSpec((BLK, width), lambda i, j, place: (block_of(i, j, place), 0)),
                pl.BlockSpec((width, total), lambda i, j, place: (0, 0)),
                pl.BlockSpec((1, BLK, rank), lambda i, j, place: (block_of(i, j, place), 0, 0)),
                pl.BlockSpec((1, rank, features), lambda i, j, place: (block_of(i, j, place), 0, 0)),
            ],
            out_specs=[
                pl.BlockSpec((1, BLK, total), lambda i, j, place: (jnp.where(i == 0, j, half - 1), 0, 0)),
                pl.BlockSpec((1, BLK, total), lambda i, j, place: (jnp.where(i == 0, 0, j), 0, 0)),
            ],
        ),
        out_shape=[shape, shape],
        compiler_params=LIMIT,
        name="keys_partials",
    )(place, tokens, frozen_weight, saved_rows, picked)


def keys_chip_sums(own, received):
    ny, block, total = own.shape

    def kernel(own_ref, received_ref, *outs):
        for d in range(ny):
            to = lax.rem(lax.axis_index("y") + d, ny)
            outs[d][...] = own_ref[to] + received_ref[to]

    return pl.pallas_call(
        kernel,
        out_shape=[jax.ShapeDtypeStruct((block, total), F32)] * ny,
        in_specs=[VMEM, VMEM],
        out_specs=[VMEM] * ny,
        compiler_params=LIMIT,
        name="keys_chip_sums",
    )(own, received)


def per_device(
    tokens, frozen_weight, saved_mid, cotangent, up_stack, block_job, block_fill, slot_of
):
    width = tokens.shape[1]
    features = cotangent.shape[1]
    rank = saved_mid.shape[1]
    nblocks = block_job.shape[0]
    slot_count = slot_of.shape[0]
    nx, nq, npair, ny = (lax.axis_size(name) for name in ADAPTER + ("y",))
    parts = nx * npair
    part, split = width // parts, rank // parts
    jobs = block_job.reshape(nblocks)
    place = jnp.stack([lax.axis_index(name) for name in SEQ]).astype(jnp.int32)

    with jax.named_scope("mid_sums"):
        own, other, picked = mid_partials(jobs, block_fill, up_stack, cotangent, saved_mid)
        own_sums, own_saved = own_parts(own)
        keep, *sent = y_first(own_sums, own_saved, shift(other, "core", 1))
        pair = [(i, i ^ 1) for i in range(ny)]
        mirror = [(i, ny - 1 - i) for i in range(ny)]
        received = [lax.ppermute(sent[0], "y", pair), lax.ppermute(sent[1], "y", mirror)]
        total, *sent = y_second(keep, sent, received)
        received = [lax.ppermute(sent[0], "y", mirror), lax.ppermute(sent[1], "y", pair)]
        mids, saved_rows = mid_grads(total, sent, received)
        mids_other = shift(mids, "core", 1)
    with jax.named_scope("terms_over_first"):
        ups, slot_rows = up_products(jobs, block_fill, slot_of, saved_rows, cotangent)
        terms = products(tokens, mids, mids_other, ups, slot_rows, parts)
        terms = lax.all_to_all(terms, FIRST, split_axis=0, concat_axis=0, tiled=True)
    with jax.named_scope("keys_core"):
        keys_own, keys_other = keys_partials(place, tokens, frozen_weight, saved_rows, picked)
        keys_parts = keys_chip_sums(keys_own, shift(keys_other, "core", 1))
        terms, keys_parts = lax.optimization_barrier((terms, keys_parts))
    with jax.named_scope("keys_y"):
        keys = keys_parts[0]
        for d in range(1, ny):
            keys = keys + shift(keys_parts[d], "y", d)
        keys = keys.astype(BF16)
    with jax.named_scope("sums_over_adapter"):
        tail = nblocks * (part + split)
        slots = terms[:, tail : tail + nblocks, 0].astype(jnp.int32)
        sums = slot_sums(slots, terms, slot_count)
        owned = lax.all_to_all(sums, ADAPTER, split_axis=0, concat_axis=0, tiled=True)
    grad_down, grad_up = finish(owned.reshape((nx, nq, npair) + owned.shape[1:]), part)
    return (keys, grad_down.reshape(1, width, rank), grad_up.reshape(1, rank, features))


def solution(mesh):
    chips = Mesh(mesh.devices.reshape(4, 4, 2, 4, 2), ("x", "zq", "zp", "y", "core"))
    return jax.shard_map(
        per_device,
        mesh=chips,
        in_specs=(
            P(ADAPTER, SEQ),
            P(SEQ, None),
            P(ADAPTER + SEQ, None),
            P(ADAPTER, SEQ),
            P(None, None, SEQ),
            P(ADAPTER, None),
            P(ADAPTER),
            P(),
        ),
        out_specs=(
            P(ADAPTER + SEQ, None),
            P(ADAPTER, SEQ, None),
            P(ADAPTER, None, SEQ),
        ),
        check_vma=False,
    )
```
